32 devices in a mesh: depth: 2 (over core), pos: 16 (over z, y, x).
Axes of the slice: x: 2, y: 2, z: 4, core: 2. Of those that a mesh axis runs over, the one named last changes fastest.
Arguments:
- object_field: bfloat16 [2, 2, 2048, 4096], P('depth', None, None, 'pos'), may hold values from -4.1875 to 4.1875
- probe: bfloat16 [4, 2, 256, 256], replicated, may hold values from -4.1875 to 4.1875
- prop_phase: float32 [256, 256], replicated, may hold values from -3.140625 to 3.140625
- measured: float32 [32, 256, 256], P('pos'), may hold values from 0 to 8
- positions: int32 [32, 2], replicated, may hold values from 0 to 3840, as said below
Outputs:
- object_grad: bfloat16 [2, 2, 2048, 4096], P('depth', None, None, 'pos')
The draws below stay inside these ranges and needn't reach their ends.
Inputs may be any that keep to these rules, and one draw needn't show every extreme that they name: `positions`: row r holds (row offset, column offset). For the block b = r // 2, column offsets lie from b * 256 to b * 256 + 255; in the last block they equal b * 256. Row offsets lie from 0 to 1792. Row 0 is (0, 0).
All inputs are finite; a program needn't handle non-finite values.
Results may differ from the reference program's by a relative error of at most 0.019.
Values may be sent and summed in bfloat16 or wider, within the bound.
No kernel may reach another device: no remote copies, remote signals or barrier semaphores. Data moves between devices by JAX's collectives and lax.ppermute only.
A program may use at most 64 MiB of HBM per device.

```python
import math
import jax
import jax.numpy as jnp
from jax import lax

NP = 256
MODES = 4
POS_DEV = 2
H = 2048
SLICES = 2
W = 4096
POSITIONS = 32
N_POS = 16


def draw_positions(key, part):
    key_rows = jax.random.fold_in(key, 11)
    key_cols = jax.random.fold_in(key, 23)
    rows_off = jax.random.randint(key_rows, (POSITIONS,), 0, H - NP + 1, dtype=jnp.int32)
    shifts = jax.random.randint(key_cols, (POSITIONS,), 0, NP, dtype=jnp.int32)
    ramp = jnp.arange(POSITIONS, dtype=jnp.int32)
    owner = ramp // POS_DEV
    shifts = jnp.where(owner == N_POS - 1, 0, shifts)
    shifts = jnp.where(ramp == 0, 0, shifts)
    rows_off = jnp.where(ramp == 0, 0, rows_off)
    cols_off = owner * NP + shifts
    return jnp.stack([rows_off, cols_off], axis=1).astype(jnp.int32)


def level_of(stream_key, shape, pieces, low, largest):
    gain, own = 1.0, jax.random.fold_in(stream_key, 6)
    for dim, blocks in pieces:
        draws = jnp.exp(jax.random.uniform(jax.random.fold_in(own, dim), (blocks,), jnp.float32, low / len(pieces), largest / len(pieces)))
        gain = gain * jnp.repeat(draws, shape[dim] // blocks).reshape([-1 if axis == dim else 1 for axis in range(len(shape))])
    return gain


def bell_draw(own_key, dims, spread, limit, pieces=(), kind=jnp.bfloat16):
    result = jax.random.normal(own_key, dims, jnp.float32) * spread
    if len(pieces) > 0:
        result = level_of(own_key, dims, pieces, -0.22, 0.18) * result
    return jnp.clip(result, min=-limit, max=limit).astype(kind)


def setup_inputs(seed: int = 0) -> dict:
    key_of = jax.random.split(jax.random.key(seed), 6)
    object_field = bell_draw(key_of[0], (SLICES, 2, H, W), 0.7, 4.1875, ((0, 2), (3, 16)))
    probe = bell_draw(key_of[1], (MODES, 2, NP, NP), 0.7, 4.1875)
    prop_phase = jnp.clip(jax.random.uniform(key_of[2], (NP, NP), jnp.float32, -3.140625, 3.140625), -3.140625, 3.140625)
    measured = jnp.clip(8.0 * jax.random.uniform(key_of[3], (POSITIONS, NP, NP), jnp.float32) ** level_of(key_of[3], (POSITIONS, NP, NP), ((0, 16),), -0.2, 0.2), 0.0, 8.0)
    positions = draw_positions(jax.random.fold_in(key_of[5], 71), 0)
    return dict(object_field=object_field, probe=probe, prop_phase=prop_phase, measured=measured, positions=positions)


def dft_tables(frame):
    ramp = jnp.arange(frame, dtype=jnp.int32)
    phases = ramp[:, None] * ramp[None, :] % frame
    angles = phases.astype(jnp.float32) * (2.0 * math.pi / frame)
    factor = 1.0 / math.sqrt(frame)
    return ((jnp.cos(angles) * factor).astype(jnp.bfloat16), (-jnp.sin(angles) * factor).astype(jnp.bfloat16))

def left_mult(table, values):
    return jnp.einsum('ab,nmbc->nmac', table.astype(jnp.float32), values.astype(jnp.float32), precision=lax.Precision.HIGHEST)

def right_mult(values, table):
    return jnp.einsum('nmab,bc->nmac', values.astype(jnp.float32), table.astype(jnp.float32), precision=lax.Precision.HIGHEST)

def transform(real_in, imag_in, fourier_table_real, fourier_table_imaginary):
    in_r = real_in.astype(jnp.bfloat16)
    in_i = imag_in.astype(jnp.bfloat16)
    mid_r = (left_mult(fourier_table_real, in_r) - left_mult(fourier_table_imaginary, in_i)).astype(jnp.bfloat16)
    mid_i = (left_mult(fourier_table_real, in_i) + left_mult(fourier_table_imaginary, in_r)).astype(jnp.bfloat16)
    out_r = right_mult(mid_r, fourier_table_real) - right_mult(mid_i, fourier_table_imaginary)
    out_i = right_mult(mid_r, fourier_table_imaginary) + right_mult(mid_i, fourier_table_real)
    return (out_r, out_i)

def forward_front(patch_r, patch_i, probe, kern_r, kern_i, fourier_table_real, fourier_table_imaginary):
    obj_r = patch_r.astype(jnp.float32)[:, None]
    obj_i = patch_i.astype(jnp.float32)[:, None]
    probe_r = probe[:, 0].astype(jnp.float32)[None]
    probe_i = probe[:, 1].astype(jnp.float32)[None]
    wave_r = probe_r * obj_r - probe_i * obj_i
    wave_i = probe_r * obj_i + probe_i * obj_r
    spectrum_real, spectrum_imaginary = transform(wave_r, wave_i, fourier_table_real, fourier_table_imaginary)
    return ((spectrum_real * kern_r - spectrum_imaginary * kern_i).astype(jnp.bfloat16), (spectrum_real * kern_i + spectrum_imaginary * kern_r).astype(jnp.bfloat16))

def backward_tail(spectrum_real, spectrum_imaginary, patch_r, patch_i, measured, fourier_table_real, fourier_table_imaginary):
    conj_i = -fourier_table_imaginary
    wave_r, wave_i = transform(spectrum_real, spectrum_imaginary, fourier_table_real, conj_i)
    obj_r = patch_r.astype(jnp.float32)[:, None]
    obj_i = patch_i.astype(jnp.float32)[:, None]
    exit_r = wave_r * obj_r - wave_i * obj_i
    exit_i = wave_r * obj_i + wave_i * obj_r
    far_r, far_i = transform(exit_r, exit_i, fourier_table_real, fourier_table_imaginary)
    intensity = lax.optimization_barrier(jnp.sum(far_r * far_r + far_i * far_i, axis=1))
    weight = ((intensity - measured) * 0.125)[:, None]
    back_r, back_i = transform(weight * far_r, weight * far_i, fourier_table_real, conj_i)
    grad_r = lax.optimization_barrier(jnp.sum(wave_r * back_r + wave_i * back_i, axis=1))
    grad_i = lax.optimization_barrier(jnp.sum(wave_r * back_i - wave_i * back_r, axis=1))
    adj_r = obj_r * back_r + obj_i * back_i
    adj_i = obj_r * back_i - obj_i * back_r
    out_r, out_i = transform(adj_r, adj_i, fourier_table_real, fourier_table_imaginary)
    return (out_r.astype(jnp.bfloat16), out_i.astype(jnp.bfloat16), grad_r, grad_i)

def back_front(adj_r, adj_i, probe, kern_r, kern_i, fourier_table_real, fourier_table_imaginary):
    cot_r = adj_r.astype(jnp.float32)
    cot_i = adj_i.astype(jnp.float32)
    turn_r = kern_r * cot_r + kern_i * cot_i
    turn_i = kern_r * cot_i - kern_i * cot_r
    wave_r, wave_i = transform(turn_r, turn_i, fourier_table_real, -fourier_table_imaginary)
    probe_r = probe[:, 0].astype(jnp.float32)[None]
    probe_i = probe[:, 1].astype(jnp.float32)[None]
    grad_r = lax.optimization_barrier(jnp.sum(probe_r * wave_r + probe_i * wave_i, axis=1))
    grad_i = lax.optimization_barrier(jnp.sum(probe_r * wave_i - probe_i * wave_r, axis=1))
    return (grad_r, grad_i)

def reference(object_field, probe, prop_phase, measured, positions):
    fourier_table_real, fourier_table_imaginary = dft_tables(NP)
    kern_r = jnp.cos(prop_phase)
    kern_i = jnp.sin(prop_phase)

    def one_position(grad, entry_value):
        frame_measured, window_offset = entry_value
        row_at = window_offset[0].astype(jnp.int32)
        col_at = window_offset[1].astype(jnp.int32)
        zero = jnp.zeros((), jnp.int32)
        first = lax.dynamic_slice(object_field[0], (zero, row_at, col_at), (2, NP, NP))
        second_slice = lax.dynamic_slice(object_field[1], (zero, row_at, col_at), (2, NP, NP))
        spectrum_real, spectrum_imaginary = forward_front(first[0][None], first[1][None], probe, kern_r, kern_i, fourier_table_real, fourier_table_imaginary)
        spectrum_grad_real, spectrum_grad_imaginary, slice_one_grad_real, slice_one_grad_imaginary = backward_tail(spectrum_real, spectrum_imaginary, second_slice[0][None], second_slice[1][None], frame_measured[None], fourier_table_real, fourier_table_imaginary)
        g0_r, g0_i = back_front(spectrum_grad_real, spectrum_grad_imaginary, probe, kern_r, kern_i, fourier_table_real, fourier_table_imaginary)
        stacked = jnp.stack([jnp.stack([g0_r[0], g0_i[0]]), jnp.stack([slice_one_grad_real[0], slice_one_grad_imaginary[0]])])
        current = lax.dynamic_slice(grad, (zero, zero, row_at, col_at), (2, 2, NP, NP))
        grad = lax.dynamic_update_slice(grad, current + stacked, (zero, zero, row_at, col_at))
        return (grad, None)
    start = jnp.zeros((SLICES, 2, H, W), jnp.float32)
    total, unused = lax.scan(one_position, start, (measured, positions))
    return total.astype(jnp.bfloat16)
```

```python
import functools
import math

import jax
import jax.numpy as jnp
import ml_dtypes
import numpy as np
from jax import lax
from jax.experimental import pallas as pl
from jax.experimental.pallas import tpu as pltpu
from jax.sharding import PartitionSpec as P

BF = jnp.bfloat16
F32 = jnp.float32
ROWS = 16
VMEM_BYTES = 48 << 20


def split_tables(frame):
    half = frame // 2
    n = np.arange(half)[:, None]
    k = np.arange(half)[None, :]
    factor = 1.0 / math.sqrt(frame)
    mats = []
    for odd in (0, 1):
        angle = (n * (2 * k + odd) % frame) * (2.0 * math.pi / frame)
        re = (np.cos(angle) * factor).astype(ml_dtypes.bfloat16)
        im = (-np.sin(angle) * factor).astype(ml_dtypes.bfloat16)
        mats.append(np.block([[re, im], [-im, re]]))
    return np.stack([mats[0], mats[1], mats[0].T, mats[1].T])


def order_table(frame):
    half = frame // 2
    q = np.arange(frame)
    source = np.where(q < half, 2 * q, 2 * (q - half) + 1)
    return (source[:, None] == np.arange(frame)[None, :]).astype(ml_dtypes.bfloat16)


def dot(a, b):
    return jnp.dot(a, b, preferred_element_type=F32)


def fwd_rows(r, i, t):
    h = r.shape[0] // 2
    up = jnp.concatenate([r[:h] + r[h:], i[:h] + i[h:]], 0).astype(BF)
    um = jnp.concatenate([r[:h] - r[h:], i[:h] - i[h:]], 0).astype(BF)
    e, o = dot(t[2], up), dot(t[3], um)
    return jnp.concatenate([e[:h], o[:h]], 0), jnp.concatenate([e[h:], o[h:]], 0)


def fwd_cols(r, i, t):
    h = r.shape[1] // 2
    up = jnp.concatenate([r[:, :h] + r[:, h:], i[:, :h] + i[:, h:]], 1).astype(BF)
    um = jnp.concatenate([r[:, :h] - r[:, h:], i[:, :h] - i[:, h:]], 1).astype(BF)
    e, o = dot(up, t[0]), dot(um, t[1])
    return jnp.concatenate([e[:, :h], o[:, :h]], 1), jnp.concatenate([e[:, h:], o[:, h:]], 1)


def inv_rows(r, i, t):
    h = r.shape[0] // 2
    e = dot(t[0], jnp.concatenate([r[:h], i[:h]], 0).astype(BF))
    o = dot(t[1], jnp.concatenate([r[h:], i[h:]], 0).astype(BF))
    s, d = e + o, e - o
    return jnp.concatenate([s[:h], d[:h]], 0), jnp.concatenate([s[h:], d[h:]], 0)


def inv_cols(r, i, t):
    h = r.shape[1] // 2
    e = dot(jnp.concatenate([r[:, :h], i[:, :h]], 1).astype(BF), t[2])
    o = dot(jnp.concatenate([r[:, h:], i[:, h:]], 1).astype(BF), t[3])
    s, d = e + o, e - o
    return jnp.concatenate([s[:, :h], d[:, :h]], 1), jnp.concatenate([s[:, h:], d[:, h:]], 1)


def fwd(r, i, t):
    return fwd_cols(*fwd_rows(r, i, t), t)


def inv(r, i, t):
    return inv_cols(*inv_rows(r, i, t), t)


def place(pos_ref, j, height, frame):
    y = pos_ref[j, 0]
    base = jnp.minimum((y >> 4) << 4, height - frame - ROWS)
    return pl.multiple_of(base, ROWS), y - base, pos_ref[j, 1] & (frame - 1)


def indices():
    depth, pos = lax.axis_index("depth"), lax.axis_index("pos")
    left = jnp.maximum(pos - 1, 0)
    return depth, pos, left


def columns(shape):
    return lax.broadcasted_iota(jnp.int32, shape, len(shape) - 1)


def rows(shape):
    return lax.broadcasted_iota(jnp.int32, shape, len(shape) - 2)


def extract_kernel(pos_ref, obj_ref, left_a, left_b, mine, other, head, tail, sems):
    _, _, height, frame = obj_ref.shape
    depth, pos, left = indices()
    jobs = [(left_a, 2 * left), (left_b, 2 * left + 1), (mine, 2 * pos + depth), (other, 2 * pos + 1 - depth)]
    started = []
    for w, (out, j) in enumerate(jobs):
        base, shift, _ = place(pos_ref, j, height, frame)
        src = obj_ref.at[0]
        copies = [
            pltpu.make_async_copy(src.at[:, pl.ds(base, ROWS)], head.at[w], sems.at[w, 0]),
            pltpu.make_async_copy(src.at[:, pl.ds(base + frame, ROWS)], tail.at[w], sems.at[w, 1]),
            pltpu.make_async_copy(
                src.at[:, pl.ds(base + ROWS, frame - ROWS)], out.at[:, ROWS:frame], sems.at[w, 2]
            ),
        ]
        for copy in copies:
            copy.start()
        started.append((copies, shift))
    for w, (out, _) in enumerate(jobs):
        copies, shift = started[w]
        copies[0].wait()
        copies[1].wait()
        first = head[w].astype(F32)
        last = tail[w].astype(F32)
        out[:, 0:ROWS] = jnp.where(rows(first.shape) >= shift, first, last).astype(BF)
    for copies, _ in started:
        copies[2].wait()


def prep_body(height, pos_ref, probe_ref, phase_ref, measured_ref, order_ref, probe_out, kern_out, measured_out):
    modes, _, frame, _ = probe_ref.shape
    depth, pos, _ = indices()
    _, row_shift, col_shift = place(pos_ref, 2 * pos + depth, height, frame)
    for m in range(modes):
        for c in range(2):
            plane = pltpu.roll(probe_ref[m, c].astype(F32), row_shift, 0)
            probe_out[m, c] = pltpu.roll(plane, col_shift, 1).astype(BF)
    order = order_ref[...]

    def reorder(x):
        for axis in (0, 1):
            total = None
            for _ in range(3):
                piece = x.astype(BF)
                x = x - piece.astype(F32)
                if axis == 0:
                    part = dot(order, piece)
                else:
                    part = lax.dot_general(
                        piece, order, (((1,), (1,)), ((), ())), preferred_element_type=F32
                    )
                total = part if total is None else total + part
            x = total
        return x

    phase = reorder(phase_ref[...])
    kern_out[0] = jnp.cos(phase)
    kern_out[1] = jnp.sin(phase)
    measured_out[...] = reorder(measured_ref[depth])


def joined(pos_ref, own_when_0, own_when_1, halo):
    frame = halo.shape[-1]
    depth, pos, _ = indices()
    shift = pos_ref[2 * pos + depth, 1] & (frame - 1)
    out = []
    for c in range(2):
        own = jnp.where(depth == 0, own_when_0[c].astype(F32), own_when_1[c].astype(F32))
        out.append(jnp.where(columns(own.shape) >= shift, own, halo[c].astype(F32)))
    return out


def front_kernel(pos_ref, own_0, own_1, halo, probe, kern, t, psi):
    obj_r, obj_i = joined(pos_ref, own_0, own_1, halo)
    for m in range(probe.shape[0]):
        pr, pi = probe[m, 0].astype(F32), probe[m, 1].astype(F32)
        r, i = fwd(pr * obj_r - pi * obj_i, pr * obj_i + pi * obj_r, t)
        kr, ki = kern[0], kern[1]
        r, i = inv(r * kr - i * ki, r * ki + i * kr, t)
        psi[m, 0] = r
        psi[m, 1] = i


def tail_kernel(pos_ref, own_0, own_1, halo, psi, measured, t, g1, adj, far):
    obj_r, obj_i = joined(pos_ref, own_0, own_1, halo)
    modes = psi.shape[0]
    inten = None
    for m in range(modes):
        pr, pi = psi[m, 0], psi[m, 1]
        r, i = fwd(pr * obj_r - pi * obj_i, pr * obj_i + pi * obj_r, t)
        far[m, 0] = r
        far[m, 1] = i
        power = r * r + i * i
        inten = power if inten is None else inten + power
    weight = (inten - measured[...]) * 0.125
    sum_r = sum_i = None
    for m in range(modes):
        r, i = inv(weight * far[m, 0], weight * far[m, 1], t)
        pr, pi = psi[m, 0], psi[m, 1]
        part_r, part_i = pr * r + pi * i, pr * i - pi * r
        sum_r = part_r if sum_r is None else sum_r + part_r
        sum_i = part_i if sum_i is None else sum_i + part_i
        adj[m, 0] = obj_r * r + obj_i * i
        adj[m, 1] = obj_r * i - obj_i * r
    g1[0] = sum_r.astype(BF)
    g1[1] = sum_i.astype(BF)


def back_kernel(adj, g1, probe, kern, t, g0, mine, other):
    depth, _, _ = indices()
    sum_r = sum_i = None
    for m in range(probe.shape[0]):
        r, i = fwd(adj[m, 0], adj[m, 1], t)
        kr, ki = kern[0], kern[1]
        r, i = inv(kr * r + ki * i, kr * i - ki * r, t)
        pr, pi = probe[m, 0].astype(F32), probe[m, 1].astype(F32)
        part_r, part_i = pr * r + pi * i, pr * i - pi * r
        sum_r = part_r if sum_r is None else sum_r + part_r
        sum_i = part_i if sum_i is None else sum_i + part_i
    for c, total in enumerate((sum_r, sum_i)):
        first = total.astype(BF)
        second = g1[c]
        g0[c] = first
        a, b = first.astype(F32), second.astype(F32)
        mine[c] = jnp.where(depth == 0, a, b).astype(BF)
        other[c] = jnp.where(depth == 0, b, a).astype(BF)


def gather_kernel(pos_ref, mine, other, spill_a0, spill_b0, spill_b1, spill_a1, out, acc):
    _, _, height, frame = out.shape
    depth, pos, left = indices()
    acc[...] = jnp.zeros_like(acc)

    def add(piece, j, spill):
        base, row_shift, col_shift = place(pos_ref, j, height, frame)

        def kept(x):
            keep = columns(x.shape) < col_shift if spill else columns(x.shape) >= col_shift
            return jnp.where(keep, x.astype(F32), 0.0)

        for c in range(2):
            head = kept(piece[c, 0:ROWS])
            below = rows(head.shape) >= row_shift
            acc[c, pl.ds(base, ROWS)] += jnp.where(below, head, 0.0)
            acc[c, pl.ds(base + frame, ROWS)] += jnp.where(below, 0.0, head)
            acc[c, pl.ds(base + ROWS, frame - ROWS)] += kept(piece[c, ROWS:frame])

    add(mine, 2 * pos + depth, False)
    add(other, 2 * pos + 1 - depth, False)

    @pl.when(jnp.logical_and(pos > 0, depth == 0))
    def _():
        add(spill_a0, 2 * left, True)
        add(spill_b0, 2 * left + 1, True)

    @pl.when(jnp.logical_and(pos > 0, depth != 0))
    def _():
        add(spill_a1, 2 * left, True)
        add(spill_b1, 2 * left + 1, True)

    for c in range(2):
        out[0, c] = acc[c].astype(BF)


def local(n_pos, object_field, probe, prop_phase, measured, positions):
    modes, _, frame, _ = probe.shape
    height = object_field.shape[2]
    both = ("depth", "pos")
    tables = jnp.asarray(split_tables(frame))
    order = jnp.asarray(order_table(frame))
    window = jax.ShapeDtypeStruct((2, frame, frame), BF)
    fields = jax.ShapeDtypeStruct((modes, 2, frame, frame), F32)
    smem = pl.BlockSpec(memory_space=pltpu.SMEM)
    vmem = pl.BlockSpec(memory_space=pltpu.VMEM)
    hbm = pl.BlockSpec(memory_space=pl.ANY)

    def call(body, name, ins, outs, scratch=(), flops=0):
        return pl.pallas_call(
            body,
            name=name,
            in_specs=ins,
            out_specs=jax.tree.map(lambda _: vmem, outs),
            out_shape=outs,
            scratch_shapes=scratch,
            compiler_params=pltpu.CompilerParams(vmem_limit_bytes=VMEM_BYTES),
            cost_estimate=pl.CostEstimate(flops=flops, bytes_accessed=4 << 20, transcendentals=0),
        )

    def dev(d, p):
        return d * n_pos + p

    def leftward(to_of):
        return [(dev(d, p + 1), dev(to, p)) for d, to in to_of for p in range(n_pos - 1)]

    def rightward(to_of):
        return [(dev(d, p), dev(to, p + 1)) for d, to in to_of for p in range(n_pos - 1)]

    swap = [(dev(d, p), dev(1 - d, p)) for d in range(2) for p in range(n_pos)]

    left_a, left_b, mine, other = call(
        extract_kernel,
        "extract",
        [smem, hbm],
        (window,) * 4,
        [
            pltpu.VMEM((4, 2, ROWS, frame), BF),
            pltpu.VMEM((4, 2, ROWS, frame), BF),
            pltpu.SemaphoreType.DMA((4, 3)),
        ],
    )(positions, object_field)

    first_a = lax.ppermute(left_a, both, leftward([(0, 0)]))
    first_b = lax.ppermute(left_b, both, leftward([(0, 1)]))
    next_a = lax.ppermute(left_a, both, swap)
    next_b = lax.ppermute(left_b, both, swap)
    partner = lax.ppermute(other, both, swap)
    second_a = lax.ppermute(next_a, both, leftward([(0, 0)]))
    second_b = lax.ppermute(next_b, both, leftward([(0, 1)]))
    depth = lax.axis_index("depth")

    probe_at, kern, measured_at = call(
        functools.partial(prep_body, height),
        "prepare",
        [smem] + [vmem] * 4,
        (
            jax.ShapeDtypeStruct(probe.shape, BF),
            jax.ShapeDtypeStruct((2, frame, frame), F32),
            jax.ShapeDtypeStruct((frame, frame), F32),
        ),
    )(positions, probe, prop_phase, measured, order)

    halo_0 = jnp.where(depth == 0, first_a, first_b)
    halo_1 = jnp.where(depth == 0, second_a, second_b)
    work = 32 * 2 * frame**3 * 2
    psi = call(front_kernel, "front", [smem] + [vmem] * 6, fields, flops=work)(
        positions, mine, partner, halo_0, probe_at, kern, tables
    )
    g1, adj = call(
        tail_kernel,
        "tail",
        [smem] + [vmem] * 6,
        (window, fields),
        [pltpu.VMEM(fields.shape, F32)],
        flops=work,
    )(positions, partner, mine, halo_1, psi, measured_at, tables)
    side_1 = lax.ppermute(g1, both, rightward([(0, 0), (1, 1)]))
    g0, keep, give = call(back_kernel, "back", [vmem] * 5, (window,) * 3, flops=work)(
        adj, g1, probe_at, kern, tables
    )
    spill_b0 = lax.ppermute(g0, both, rightward([(1, 0)]))
    spill_a0 = lax.ppermute(g0, both, rightward([(0, 0)]))
    given = lax.ppermute(give, both, swap)
    spill_a1 = lax.ppermute(side_1, both, swap)
    return call(
        gather_kernel,
        "gather",
        [smem] + [vmem] * 6,
        jax.ShapeDtypeStruct(object_field.shape, BF),
        [pltpu.VMEM((2, height, frame), F32)],
    )(positions, keep, given, spill_a0, spill_b0, side_1, spill_a1)


def solution(mesh):
    placed = (P("depth", None, None, "pos"), P(), P(), P("pos", None, None), P())
    return jax.shard_map(
        functools.partial(local, mesh.shape["pos"]),
        mesh=mesh,
        in_specs=placed,
        out_specs=P("depth", None, None, "pos"),
        check_vma=False,
    )
```

```python
import functools
import math

import jax
import jax.numpy as jnp
import ml_dtypes
import numpy as np
from jax import lax
from jax.experimental import pallas as pl
from jax.experimental.pallas import tpu as pltpu
from jax.sharding import PartitionSpec as P

BF = jnp.bfloat16
F32 = jnp.float32
ROWS = 16
VMEM_BYTES = 20 << 20
LIGHT, HEAVY = 1000, 4 << 30
EXTRACT_BYTES = 52 << 20


def split_tables(frame):
    half = frame // 2
    n = np.arange(half)[:, None]
    k = np.arange(half)[None, :]
    factor = 1.0 / math.sqrt(frame)
    mats = []
    for odd in (0, 1):
        angle = (n * (2 * k + odd) % frame) * (2.0 * math.pi / frame)
        re = (np.cos(angle) * factor).astype(ml_dtypes.bfloat16)
        im = (-np.sin(angle) * factor).astype(ml_dtypes.bfloat16)
        mats.append(np.block([[re, im], [-im, re]]))
    return np.stack([mats[0], mats[1], mats[0].T, mats[1].T])


def dot(a, b):
    return jnp.dot(a, b, preferred_element_type=F32)


def load_f32(ref, *index):
    return ref[index].astype(F32)


def store_sums(u, m, lanes, low, high):
    h = low[0].shape[0]
    for c in range(2):
        u[m, 0, c * h : (c + 1) * h, lanes] = (low[c] + high[c]).astype(BF)
        u[m, 1, c * h : (c + 1) * h, lanes] = (low[c] - high[c]).astype(BF)


def rows_fwd(u, v, m, t):
    h = t.shape[-1] // 2
    for k in range(2):
        x = dot(t[2 + k], u[m, k])
        at = pl.ds(k * h, h)
        for c in range(2):
            low, high = x[c * h : (c + 1) * h, :h], x[c * h : (c + 1) * h, h:]
            v[m, at, c * h : (c + 1) * h] = (low + high).astype(BF)
            v[m, at, (2 + c) * h : (3 + c) * h] = (low - high).astype(BF)


def rows_inv(u, v, m, t):
    h = t.shape[-1] // 2
    e, o = dot(t[0], u[m, 0]), dot(t[1], u[m, 1])
    for k, x in enumerate((e + o, e - o)):
        at = pl.ds(k * h, h)
        for c in range(2):
            v[m, at, c * h : (c + 1) * h] = x[c * h : (c + 1) * h, :h].astype(BF)
            v[m, at, (2 + c) * h : (3 + c) * h] = x[c * h : (c + 1) * h, h:].astype(BF)


def cols(v, m, t, inverse, sink):
    h = t.shape[-1] // 2
    k = 2 if inverse else 0
    e, o = dot(v[m, :, : 2 * h], t[k]), dot(v[m, :, 2 * h :], t[k + 1])
    if inverse:
        e, o = e + o, e - o
    for b, x in enumerate((e, o)):
        sink(m, b, (x[:h, :h], x[:h, h:]), (x[h:, :h], x[h:, h:]))


def block(h, a):
    return slice(a * h, (a + 1) * h)


def store_spectrum(u, m, a, b, r, i):
    h = r.shape[0]
    u[m, a, 0:h, block(h, b)] = r.astype(BF)
    u[m, a, h : 2 * h, block(h, b)] = i.astype(BF)


def place(pos_ref, j, height, frame):
    y = pos_ref[0, j]
    base = jnp.minimum((y >> 4) << 4, height - frame - ROWS)
    return pl.multiple_of(base, ROWS), y - base, pos_ref[1, j] & (frame - 1)


def indices():
    depth, pos = lax.axis_index("depth"), lax.axis_index("pos")
    left = jnp.maximum(pos - 1, 0)
    return depth, pos, left


def columns(shape):
    return lax.broadcasted_iota(jnp.int32, shape, len(shape) - 1)


def rows(shape):
    return lax.broadcasted_iota(jnp.int32, shape, len(shape) - 2)


def extract_kernel(pos_ref, obj_ref, left_a, left_b, mine, other, ends, sems):
    _, _, height, frame = obj_ref.shape
    depth, pos, left = indices()
    src = obj_ref.at[0]
    jobs = []
    for w, (out, j) in enumerate(
        [
            (left_a, 2 * left),
            (left_b, 2 * left + 1),
            (mine, 2 * pos + depth),
            (other, 2 * pos + 1 - depth),
        ]
    ):
        base, shift, _ = place(pos_ref, j, height, frame)
        body = pltpu.make_async_copy(src.at[:, pl.ds(base, frame)], out, sems.at[w, 0])
        end = pltpu.make_async_copy(src.at[:, pl.ds(base + frame, ROWS)], ends.at[w], sems.at[w, 1])
        end.start()
        body.start()
        jobs.append((out, body, end, shift))
    for w, (out, body, end, shift) in enumerate(jobs):
        end.wait()
        body.wait()
        upper, lower = out[:, 0:ROWS].astype(F32), ends[w].astype(F32)
        out[:, 0:ROWS] = jnp.where(rows(upper.shape) >= shift, upper, lower).astype(BF)


def cos_sin(x):
    x = x - jnp.floor(x * (0.5 / math.pi) + 0.5) * (2.0 * math.pi)
    t = 0.5 * x
    z = t * t
    sine = t * (1.0 + z * (-1 / 6 + z * (1 / 120 + z * (-1 / 5040 + z * (1 / 362880 - z / 39916800)))))
    cosine = 1.0 + z * (
        -1 / 2 + z * (1 / 24 + z * (-1 / 720 + z * (1 / 40320 + z * (-1 / 3628800 + z / 479001600))))
    )
    return 1.0 - 2.0 * sine * sine, 2.0 * sine * cosine


def prepare_kernel(height, pos_ref, probe_ref, phase_ref, measured_ref, probe_out, kern_out, measured_out, shift_out):
    modes, _, frame, _ = probe_ref.shape
    depth, pos, _ = indices()
    half = frame // 2
    _, row_shift, col_shift = place(pos_ref, 2 * pos + depth, height, frame)
    shift_out[...] = jnp.full(shift_out.shape, col_shift, jnp.int32)
    down = lax.broadcasted_iota(jnp.int32, (frame, frame), 0)
    across = lax.broadcasted_iota(jnp.int32, (frame, frame), 1)

    def chosen(where):
        return jnp.where(where, 1.0, 0.0).astype(BF)

    def even_odd(n):
        return jnp.where(n < half, 2 * n, 2 * (n - half) + 1)

    order, order_t = chosen(across == even_odd(down)), chosen(down == even_odd(across))
    turn = chosen(across == ((down - row_shift) & (frame - 1)))

    def reorder(x):
        for axis in (0, 1):
            high = x.astype(BF)
            low = (x - high.astype(F32)).astype(BF)
            if axis == 0:
                x = dot(order, high) + dot(order, low)
            else:
                x = dot(high, order_t) + dot(low, order_t)
        return x

    kern_out[0], kern_out[1] = cos_sin(reorder(phase_ref[...]))
    for m in range(modes):
        for c in range(2):
            plane = pltpu.roll(probe_ref[m, c].astype(F32), col_shift, 1).astype(BF)
            probe_out[m, c] = dot(turn, plane).astype(BF)
    measured_out[...] = reorder(measured_ref[depth])


def join(shift, obj, own, halo):
    for c in range(2):
        near = own[c].astype(F32)
        obj[c] = jnp.where(columns(near.shape) >= shift[0:1], near, halo[c].astype(F32))


def front_steps(obj, probe, kern, t, psi, u, v):
    h = t.shape[-1] // 2
    modes = range(probe.shape[0])
    for m in modes:
        halves = []
        for a in range(2):
            at = block(h, a)
            pr, pi = load_f32(probe, m, 0, at), load_f32(probe, m, 1, at)
            qr, qi = obj[0, at], obj[1, at]
            halves.append((pr * qr - pi * qi, pr * qi + pi * qr))
        store_sums(u, m, slice(None), *halves)
    for m in modes:
        rows_fwd(u, v, m, t)

    def spectrum(m, b, *halves):
        for a, (r, i) in enumerate(halves):
            kr, ki = kern[0, block(h, a), block(h, b)], kern[1, block(h, a), block(h, b)]
            store_spectrum(u, m, a, b, r * kr - i * ki, r * ki + i * kr)

    def wave(m, b, *halves):
        for a, (r, i) in enumerate(halves):
            psi[m, 0, block(h, a), block(h, b)] = r
            psi[m, 1, block(h, a), block(h, b)] = i

    for m in modes:
        cols(v, m, t, False, spectrum)
    for m in modes:
        rows_inv(u, v, m, t)
    for m in modes:
        cols(v, m, t, True, wave)


def tail_steps(obj, psi, measured, t, g1, adj, far, inten, total, u, v):
    h = t.shape[-1] // 2
    modes = range(psi.shape[0])
    for m in modes:
        halves = []
        for a in range(2):
            at = block(h, a)
            pr, pi, qr, qi = psi[m, 0, at], psi[m, 1, at], obj[0, at], obj[1, at]
            halves.append((pr * qr - pi * qi, pr * qi + pi * qr))
        store_sums(u, m, slice(None), *halves)
    for m in modes:
        rows_fwd(u, v, m, t)

    def detect(m, b, *halves):
        for a, (r, i) in enumerate(halves):
            at = (block(h, a), block(h, b))
            far[(m, 0) + at] = r
            far[(m, 1) + at] = i
            power = r * r + i * i
            inten[at] = power if m == 0 else inten[at] + power

    for m in modes:
        cols(v, m, t, False, detect)
    for a in range(2):
        for b in range(2):
            at = (block(h, a), block(h, b))
            weight = (inten[at] - measured[at].astype(F32)) * 0.125
            for m in modes:
                store_spectrum(u, m, a, b, weight * far[(m, 0) + at], weight * far[(m, 1) + at])
    for m in modes:
        rows_inv(u, v, m, t)
    last = psi.shape[0] - 1

    def back(m, b, *halves):
        adjoint = []
        for a, (r, i) in enumerate(halves):
            at = (block(h, a), block(h, b))
            pr, pi = psi[(m, 0) + at], psi[(m, 1) + at]
            add_up(g1, total, at, m == 0, m == last, pr * r + pi * i, pr * i - pi * r)
            qr, qi = obj[(0,) + at], obj[(1,) + at]
            adjoint.append((qr * r + qi * i, qr * i - qi * r))
        store_sums(adj, m, block(h, b), *adjoint)

    for m in modes:
        cols(v, m, t, True, back)


def back_steps(adj, probe, kern, t, g0, total, u, v):
    h = t.shape[-1] // 2
    modes = range(probe.shape[0])
    for m in modes:
        rows_fwd(adj, v, m, t)

    def spectrum(m, b, *halves):
        for a, (r, i) in enumerate(halves):
            kr, ki = kern[0, block(h, a), block(h, b)], kern[1, block(h, a), block(h, b)]
            store_spectrum(u, m, a, b, kr * r + ki * i, kr * i - ki * r)

    for m in modes:
        cols(v, m, t, False, spectrum)
    for m in modes:
        rows_inv(u, v, m, t)
    last = probe.shape[0] - 1

    def back(m, b, *halves):
        for a, (r, i) in enumerate(halves):
            at = (block(h, a), block(h, b))
            pr, pi = load_f32(probe, m, 0, *at), load_f32(probe, m, 1, *at)
            add_up(g0, total, at, m == 0, m == last, pr * r + pi * i, pr * i - pi * r)

    for m in modes:
        cols(v, m, t, True, back)


def add_up(out, total, at, first, last, *parts):
    for c, part in enumerate(parts):
        if not first:
            part = part + total[(c,) + at]
        if last:
            out[(c,) + at] = part.astype(BF)
        else:
            total[(c,) + at] = part


def front_kernel(core, shift, own, halo, probe, kern, t, psi, obj, u, v):
    @pl.when(lax.axis_index("depth") == core)
    def _():
        join(shift, obj, own, halo)
        front_steps(obj, probe, kern, t, psi, u, v)


def tail_kernel(core, shift, own, halo, psi, measured, t, g1, adj, obj, far, inten, total, u, v):
    @pl.when(lax.axis_index("depth") == core)
    def _():
        join(shift, obj, own, halo)
        tail_steps(obj, psi, measured, t, g1, adj, far, inten, total, u, v)


def back_a_kernel(adj, probe, kern, t, g0, total, u, v):
    depth, _, _ = indices()

    @pl.when(depth == 0)
    def _():
        back_steps(adj, probe, kern, t, g0, total, u, v)


def back_b_kernel(adj, g1_a, probe, kern, t, give, total, u, v):
    depth, _, _ = indices()

    @pl.when(depth == 0)
    def _():
        give[...] = g1_a[...]

    @pl.when(depth != 0)
    def _():
        back_steps(adj, probe, kern, t, give, total, u, v)


def add_window(acc, pos_ref, piece, j, spill):
    _, height, frame = acc.shape
    base, row_shift, col_shift = place(pos_ref, j, height, frame)

    def kept(x):
        keep = columns(x.shape) < col_shift if spill else columns(x.shape) >= col_shift
        return jnp.where(keep, x.astype(F32), 0.0)

    for c in range(2):
        part = piece[c] if isinstance(piece, tuple) else piece.at[c]
        head = kept(part[0:ROWS])
        below = rows(head.shape) >= row_shift
        acc[c, pl.ds(base, ROWS)] += jnp.where(below, head, 0.0)
        acc[c, pl.ds(base + frame, ROWS)] += jnp.where(below, 0.0, head)
        acc[c, pl.ds(base + ROWS, frame - ROWS)] += kept(part[ROWS:frame])


def begin_kernel(pos_ref, g0_a, g1_b, acc):
    depth, pos, _ = indices()
    acc[...] = jnp.zeros_like(acc)
    for d, own in ((0, g0_a), (1, g1_b)):

        @pl.when(depth == d)
        def _():
            add_window(acc, pos_ref, own, 2 * pos + d, False)


def add_kernel(pos_ref, acc_in, spill_0, spill_1, acc):
    del acc_in
    depth, pos, left = indices()
    for d, spill in ((0, spill_0), (1, spill_1)):

        @pl.when(jnp.logical_and(pos > 0, depth == d))
        def _():
            add_window(acc, pos_ref, spill, 2 * left + d, True)


def gather_kernel(pos_ref, acc_in, spill_0, spill_1, given, out, acc, stage, sems):
    del acc_in
    _, height, frame = acc.shape
    depth, pos, left = indices()
    add_window(acc, pos_ref, given, 2 * pos + 1 - depth, False)
    for d, spill in ((0, spill_0), (1, spill_1)):

        @pl.when(jnp.logical_and(pos > 0, depth == d))
        def _():
            add_window(acc, pos_ref, spill, 2 * left + 1 - d, True)

    copies = []
    for c in range(2):
        for n, first in enumerate(range(0, height, frame)):
            at = slice(first, first + frame)
            stage[c, at] = acc[c, at].astype(BF)
            copy = pltpu.make_async_copy(stage.at[c, at], out.at[0, c, at], sems.at[c, n])
            copy.start()
            copies.append(copy)
    for copy in copies:
        copy.wait()


def local(n_pos, object_field, probe, prop_phase, measured, positions):
    modes, _, frame, _ = probe.shape
    height = object_field.shape[2]
    both = ("depth", "pos")
    tables = jnp.asarray(split_tables(frame))
    window = jax.ShapeDtypeStruct((2, frame, frame), BF)
    fields = jax.ShapeDtypeStruct((modes, 2, frame, frame), F32)
    smem = pl.BlockSpec(memory_space=pltpu.SMEM)
    vmem = pl.BlockSpec(memory_space=pltpu.VMEM)
    hbm = pl.BlockSpec(memory_space=pltpu.HBM)

    def call(body, name, ins, outs, scratch=(), cost=LIGHT, out_specs=None, aliases=None, vmem_bytes=VMEM_BYTES):
        return pl.pallas_call(
            body,
            name=name,
            in_specs=ins,
            out_specs=jax.tree.map(lambda _: vmem, outs) if out_specs is None else out_specs,
            out_shape=outs,
            input_output_aliases=aliases or {},
            scratch_shapes=scratch,
            compiler_params=pltpu.CompilerParams(vmem_limit_bytes=vmem_bytes),
            cost_estimate=pl.CostEstimate(flops=cost, bytes_accessed=1000, transcendentals=0),
        )

    def dev(d, p):
        return d * n_pos + p

    def leftward(to_of):
        return [(dev(d, p + 1), dev(to, p)) for d, to in to_of for p in range(n_pos - 1)]

    def rightward(to_of):
        return [(dev(d, p), dev(to, p + 1)) for d, to in to_of for p in range(n_pos - 1)]

    positions = positions.T
    def send(name, x, pairs):
        with jax.named_scope(name):
            return lax.ppermute(x, both, pairs)

    swap = [(dev(d, p), dev(1 - d, p)) for d in range(2) for p in range(n_pos)]

    left_a, left_b, mine, other = call(
        extract_kernel,
        "extract",
        [smem, hbm],
        (window,) * 4,
        [pltpu.VMEM((4, 2, ROWS, frame), BF), pltpu.SemaphoreType.DMA((4, 2))],
        vmem_bytes=EXTRACT_BYTES,
    )(positions, object_field)
    first_a = send("first_a", left_a, leftward([(0, 0)]))
    second_a = send("second_a", left_a, leftward([(1, 0)]))
    partner = send("partner", other, swap)
    left_b, partner = lax.optimization_barrier((left_b, partner))
    first_b = send("first_b", left_b, leftward([(0, 1)]))
    second_b = send("second_b", left_b, leftward([(1, 1)]))
    probe_at, kern, measured_at, shift = call(
        functools.partial(prepare_kernel, height),
        "prepare",
        [smem] + [vmem] * 3,
        (
            jax.ShapeDtypeStruct(probe.shape, BF),
            jax.ShapeDtypeStruct((2, frame, frame), F32),
            jax.ShapeDtypeStruct((frame, frame), F32),
            jax.ShapeDtypeStruct((8, frame), jnp.int32),
        ),
    )(positions, probe, prop_phase, measured)

    packed = [pltpu.VMEM((modes, 2, frame, frame), BF), pltpu.VMEM((modes, frame, 2 * frame), BF)]
    sums_of = jax.ShapeDtypeStruct((modes, 2, frame, frame), BF)
    pair = pltpu.VMEM((2, frame, frame), F32)
    deep = [pair, pltpu.VMEM(fields.shape, F32), pltpu.VMEM((frame, frame), F32), pair] + packed
    def front(core, own, halo):
        body = functools.partial(front_kernel, core)
        return call(body, "front" + "ab"[core], [vmem] * 6, fields, [pair] + packed)(
            shift, own, halo, probe_at, kern, tables
        )

    def tail(core, own, halo, psi):
        body = functools.partial(tail_kernel, core)
        return call(body, "tail" + "ab"[core], [vmem] * 6, (window, sums_of), deep)(
            shift, own, halo, psi, measured_at, tables
        )

    barrier = lax.optimization_barrier
    psi_a = front(0, mine, first_a)
    first_b, psi_a = barrier((first_b, psi_a))
    psi_b = front(1, partner, first_b)
    psi_a, psi_b = barrier((psi_a, psi_b))
    g1_a, adj_a = tail(0, partner, second_a, psi_a)
    side_a = send("side_a", g1_a, rightward([(0, 0)]))
    psi_b, g1_a = barrier((psi_b, g1_a))
    g1_b, adj_b = tail(1, mine, second_b, psi_b)
    spill_b1 = send("spill_b1", g1_b, rightward([(1, 1)]))
    adj_a, g1_b = barrier((adj_a, g1_b))
    g0_a = call(back_a_kernel, "backa", [vmem] * 4, window, [pair] + packed)(
        adj_a, probe_at, kern, tables
    )
    spill_a0 = send("spill_a0", g0_a, rightward([(0, 0)]))
    adj_b, g0_a = barrier((adj_b, g0_a))
    give = call(back_b_kernel, "backb", [vmem] * 5, window, [pair] + packed)(
        adj_b, g1_a, probe_at, kern, tables
    )
    spill_b0 = send("spill_b0", give, rightward([(1, 0)]))
    sums = jax.ShapeDtypeStruct((2, height, frame), F32)
    total = call(begin_kernel, "begin", [smem] + [vmem] * 2, sums)(positions, g0_a, g1_b)
    total, give, side_a = barrier((total, give, side_a))
    given = send("given", give, swap)
    spill_a1 = send("spill_a1", side_a, swap)
    total = call(add_kernel, "add", [smem] + [vmem] * 3, sums, aliases={1: 0}, cost=HEAVY)(
        positions, total, spill_a0, spill_b1
    )
    out, _ = call(
        gather_kernel,
        "gather",
        [smem] + [vmem] * 4,
        (jax.ShapeDtypeStruct(object_field.shape, BF), sums),
        [pltpu.VMEM((2, height, frame), BF), pltpu.SemaphoreType.DMA((2, height // frame))],
        out_specs=(hbm, vmem),
        aliases={1: 1},
    )(positions, total, spill_b0, spill_a1, given)
    return out


def solution(mesh):
    placed = (P("depth", None, None, "pos"), P(), P(), P("pos", None, None), P())
    return jax.shard_map(
        functools.partial(local, mesh.shape["pos"]),
        mesh=mesh,
        in_specs=placed,
        out_specs=P("depth", None, None, "pos"),
        check_vma=False,
    )
```

```python
import functools
import math

import jax
import jax.numpy as jnp
import ml_dtypes
import numpy as np
from jax import lax
from jax.experimental import pallas as pl
from jax.experimental.pallas import tpu as pltpu
from jax.sharding import PartitionSpec as P

BF = jnp.bfloat16
F32 = jnp.float32
ROWS = 16
VMEM_BYTES = 20 << 20
LIGHT, HEAVY = 1000, 4 << 30
EXTRACT_BYTES = 52 << 20


def split_tables(frame):
    half = frame // 2
    n = np.arange(half)[:, None]
    k = np.arange(half)[None, :]
    factor = 1.0 / math.sqrt(frame)
    mats = []
    for odd in (0, 1):
        angle = (n * (2 * k + odd) % frame) * (2.0 * math.pi / frame)
        re = (np.cos(angle) * factor).astype(ml_dtypes.bfloat16)
        im = (-np.sin(angle) * factor).astype(ml_dtypes.bfloat16)
        mats.append(np.block([[re, im], [-im, re]]))
    return np.stack([mats[0], mats[1], mats[0].T, mats[1].T])


def dot(a, b):
    return jnp.dot(a, b, preferred_element_type=F32)


def load_f32(ref, *index):
    return ref[index].astype(F32)


def store_sums(u, m, lanes, low, high):
    h = low[0].shape[0]
    for c in range(2):
        u[m, 0, c * h : (c + 1) * h, lanes] = (low[c] + high[c]).astype(BF)
        u[m, 1, c * h : (c + 1) * h, lanes] = (low[c] - high[c]).astype(BF)


def rows_fwd(u, v, m, t):
    h = t.shape[-1] // 2
    for k in range(2):
        x = dot(t[2 + k], u[m, k])
        at = pl.ds(k * h, h)
        for c in range(2):
            low, high = x[c * h : (c + 1) * h, :h], x[c * h : (c + 1) * h, h:]
            v[m, at, c * h : (c + 1) * h] = (low + high).astype(BF)
            v[m, at, (2 + c) * h : (3 + c) * h] = (low - high).astype(BF)


def rows_inv(u, v, m, t):
    h = t.shape[-1] // 2
    e, o = dot(t[0], u[m, 0]), dot(t[1], u[m, 1])
    for k, x in enumerate((e + o, e - o)):
        at = pl.ds(k * h, h)
        for c in range(2):
            v[m, at, c * h : (c + 1) * h] = x[c * h : (c + 1) * h, :h].astype(BF)
            v[m, at, (2 + c) * h : (3 + c) * h] = x[c * h : (c + 1) * h, h:].astype(BF)


def cols(v, m, t, inverse, sink):
    h = t.shape[-1] // 2
    k = 2 if inverse else 0
    e, o = dot(v[m, :, : 2 * h], t[k]), dot(v[m, :, 2 * h :], t[k + 1])
    if inverse:
        e, o = e + o, e - o
    for b, x in enumerate((e, o)):
        sink(m, b, (x[:h, :h], x[:h, h:]), (x[h:, :h], x[h:, h:]))


def block(h, a):
    return slice(a * h, (a + 1) * h)


def store_spectrum(u, m, a, b, r, i):
    h = r.shape[0]
    u[m, a, 0:h, block(h, b)] = r.astype(BF)
    u[m, a, h : 2 * h, block(h, b)] = i.astype(BF)


def pick(pos_ref, row, j):
    x = pos_ref[row : row + 1].astype(F32)
    return jnp.sum(jnp.where(columns(x.shape) == j, x, 0.0)).astype(jnp.int32)


def place(pos_ref, j, height, frame):
    y = pick(pos_ref, 0, j)
    base = jnp.minimum((y >> 4) << 4, height - frame - ROWS)
    return pl.multiple_of(base, ROWS), y - base, pick(pos_ref, 1, j) & (frame - 1)


def indices():
    depth, pos = lax.axis_index("depth"), lax.axis_index("pos")
    left = jnp.maximum(pos - 1, 0)
    return depth, pos, left


def columns(shape):
    return lax.broadcasted_iota(jnp.int32, shape, len(shape) - 1)


def rows(shape):
    return lax.broadcasted_iota(jnp.int32, shape, len(shape) - 2)


def extract_kernel(pos_ref, obj_ref, left_a, left_b, mine, pair, ends, sems):
    _, _, height, frame = obj_ref.shape
    depth, pos, left = indices()
    src = obj_ref.at[0]
    jobs = []
    for w, (outs, j) in enumerate(
        [
            ((left_a,), 2 * left),
            ((left_b, pair.at[0]), 2 * left + 1),
            ((pair.at[1],), 2 * pos + 1 - depth),
            ((mine,), 2 * pos + depth),
        ]
    ):
        base, shift, _ = place(pos_ref, j, height, frame)
        body = pltpu.make_async_copy(src.at[:, pl.ds(base, frame)], outs[0], sems.at[w, 0])
        end = pltpu.make_async_copy(src.at[:, pl.ds(base + frame, ROWS)], ends.at[w], sems.at[w, 1])
        end.start()
        body.start()
        jobs.append((outs, body, end, shift))
    for w, (outs, body, end, shift) in enumerate(jobs):
        end.wait()
        body.wait()
        upper, lower = outs[0][:, 0:ROWS].astype(F32), ends[w].astype(F32)
        outs[0][:, 0:ROWS] = jnp.where(rows(upper.shape) >= shift, upper, lower).astype(BF)
        for copy in outs[1:]:
            copy[...] = outs[0][...]


def cos_sin(x):
    x = x - jnp.floor(x * (0.5 / math.pi) + 0.5) * (2.0 * math.pi)
    t = 0.5 * x
    z = t * t
    sine = t * (1.0 + z * (-1 / 6 + z * (1 / 120 + z * (-1 / 5040 + z * (1 / 362880 - z / 39916800)))))
    cosine = 1.0 + z * (
        -1 / 2 + z * (1 / 24 + z * (-1 / 720 + z * (1 / 40320 + z * (-1 / 3628800 + z / 479001600))))
    )
    return 1.0 - 2.0 * sine * sine, 2.0 * sine * cosine


def prepare_kernel(height, pos_ref, probe_ref, phase_ref, measured_ref, probe_out, kern_out, measured_out, shift_out):
    modes, _, frame, _ = probe_ref.shape
    depth, pos, _ = indices()
    half = frame // 2
    _, row_shift, col_shift = place(pos_ref, 2 * pos + depth, height, frame)
    shift_out[...] = jnp.full(shift_out.shape, col_shift, jnp.int32)
    down = lax.broadcasted_iota(jnp.int32, (frame, frame), 0)
    across = lax.broadcasted_iota(jnp.int32, (frame, frame), 1)

    def chosen(where):
        return jnp.where(where, 1.0, 0.0).astype(BF)

    def even_odd(n):
        return jnp.where(n < half, 2 * n, 2 * (n - half) + 1)

    order, order_t = chosen(across == even_odd(down)), chosen(down == even_odd(across))
    turn = chosen(across == ((down - row_shift) & (frame - 1)))

    def reorder(x):
        for axis in (0, 1):
            high = x.astype(BF)
            low = (x - high.astype(F32)).astype(BF)
            if axis == 0:
                x = dot(order, high) + dot(order, low)
            else:
                x = dot(high, order_t) + dot(low, order_t)
        return x

    kern_out[0], kern_out[1] = cos_sin(reorder(phase_ref[...]))
    for m in range(modes):
        for c in range(2):
            plane = pltpu.roll(probe_ref[m, c].astype(F32), col_shift, 1).astype(BF)
            probe_out[m, c] = dot(turn, plane).astype(BF)
    measured_out[...] = reorder(measured_ref[depth])


def join(shift, obj, own, halo):
    for c in range(2):
        near = own[c].astype(F32)
        obj[c] = jnp.where(columns(near.shape) >= shift[0:1], near, halo[c].astype(F32))


def front_steps(obj, probe, kern, t, psi, u, v):
    h = t.shape[-1] // 2
    modes = range(probe.shape[0])
    for m in modes:
        halves = []
        for a in range(2):
            at = block(h, a)
            pr, pi = load_f32(probe, m, 0, at), load_f32(probe, m, 1, at)
            qr, qi = obj[0, at], obj[1, at]
            halves.append((pr * qr - pi * qi, pr * qi + pi * qr))
        store_sums(u, m, slice(None), *halves)
    for m in modes:
        rows_fwd(u, v, m, t)

    def spectrum(m, b, *halves):
        for a, (r, i) in enumerate(halves):
            kr, ki = kern[0, block(h, a), block(h, b)], kern[1, block(h, a), block(h, b)]
            store_spectrum(u, m, a, b, r * kr - i * ki, r * ki + i * kr)

    def wave(m, b, *halves):
        for a, (r, i) in enumerate(halves):
            psi[m, 0, block(h, a), block(h, b)] = r
            psi[m, 1, block(h, a), block(h, b)] = i

    for m in modes:
        cols(v, m, t, False, spectrum)
    for m in modes:
        rows_inv(u, v, m, t)
    for m in modes:
        cols(v, m, t, True, wave)


def tail_steps(obj, psi, measured, t, g1, adj, far, inten, total, u, v):
    h = t.shape[-1] // 2
    modes = range(psi.shape[0])
    for m in modes:
        halves = []
        for a in range(2):
            at = block(h, a)
            pr, pi, qr, qi = psi[m, 0, at], psi[m, 1, at], obj[0, at], obj[1, at]
            halves.append((pr * qr - pi * qi, pr * qi + pi * qr))
        store_sums(u, m, slice(None), *halves)
    for m in modes:
        rows_fwd(u, v, m, t)

    def detect(m, b, *halves):
        for a, (r, i) in enumerate(halves):
            at = (block(h, a), block(h, b))
            far[(m, 0) + at] = r
            far[(m, 1) + at] = i
            power = r * r + i * i
            inten[at] = power if m == 0 else inten[at] + power

    for m in modes:
        cols(v, m, t, False, detect)
    for a in range(2):
        for b in range(2):
            at = (block(h, a), block(h, b))
            weight = (inten[at] - measured[at].astype(F32)) * 0.125
            for m in modes:
                store_spectrum(u, m, a, b, weight * far[(m, 0) + at], weight * far[(m, 1) + at])
    for m in modes:
        rows_inv(u, v, m, t)
    last = psi.shape[0] - 1

    def back(m, b, *halves):
        adjoint = []
        for a, (r, i) in enumerate(halves):
            at = (block(h, a), block(h, b))
            pr, pi = psi[(m, 0) + at], psi[(m, 1) + at]
            add_up(g1, total, at, m == 0, m == last, pr * r + pi * i, pr * i - pi * r)
            qr, qi = obj[(0,) + at], obj[(1,) + at]
            adjoint.append((qr * r + qi * i, qr * i - qi * r))
        store_sums(adj, m, block(h, b), *adjoint)

    for m in modes:
        cols(v, m, t, True, back)


def back_steps(adj, probe, kern, t, g0, total, u, v):
    h = t.shape[-1] // 2
    modes = range(probe.shape[0])
    for m in modes:
        rows_fwd(adj, v, m, t)

    def spectrum(m, b, *halves):
        for a, (r, i) in enumerate(halves):
            kr, ki = kern[0, block(h, a), block(h, b)], kern[1, block(h, a), block(h, b)]
            store_spectrum(u, m, a, b, kr * r + ki * i, kr * i - ki * r)

    for m in modes:
        cols(v, m, t, False, spectrum)
    for m in modes:
        rows_inv(u, v, m, t)
    last = probe.shape[0] - 1

    def back(m, b, *halves):
        for a, (r, i) in enumerate(halves):
            at = (block(h, a), block(h, b))
            pr, pi = load_f32(probe, m, 0, *at), load_f32(probe, m, 1, *at)
            add_up(g0, total, at, m == 0, m == last, pr * r + pi * i, pr * i - pi * r)

    for m in modes:
        cols(v, m, t, True, back)


def add_up(out, total, at, first, last, *parts):
    for c, part in enumerate(parts):
        if not first:
            part = part + total[(c,) + at]
        if last:
            out[(c,) + at] = part.astype(BF)
        else:
            total[(c,) + at] = part


def front_kernel(core, shift, own, halo, probe, kern, t, psi, obj, u, v):
    @pl.when(lax.axis_index("depth") == core)
    def _():
        join(shift, obj, own if core == 0 else own.at[1], halo)
        front_steps(obj, probe, kern, t, psi, u, v)


def tail_kernel(core, shift, own, halo, psi, measured, t, g1, adj, obj, far, inten, total, u, v):
    @pl.when(lax.axis_index("depth") == core)
    def _():
        join(shift, obj, own if core == 1 else own.at[1], halo)
        tail_steps(obj, psi, measured, t, g1, adj, far, inten, total, u, v)


def back_a_kernel(adj, g1, probe, kern, t, out, total, u, v):
    @pl.when(lax.axis_index("depth") == 0)
    def _():
        back_steps(adj, probe, kern, t, out.at[0], total, u, v)
        out[1] = g1[...]


def back_b_kernel(adj, g1_a, probe, kern, t, give, total, u, v):
    depth, _, _ = indices()

    @pl.when(depth == 0)
    def _():
        give[...] = g1_a[...]

    @pl.when(depth != 0)
    def _():
        back_steps(adj, probe, kern, t, give, total, u, v)


def add_window(acc, pos_ref, piece, j, spill):
    _, height, frame = acc.shape
    base, row_shift, col_shift = place(pos_ref, j, height, frame)

    def kept(x):
        keep = columns(x.shape) < col_shift if spill else columns(x.shape) >= col_shift
        return jnp.where(keep, x.astype(F32), 0.0)

    for c in range(2):
        part = piece[c] if isinstance(piece, tuple) else piece.at[c]
        head = kept(part[0:ROWS])
        below = rows(head.shape) >= row_shift
        acc[c, pl.ds(base, ROWS)] += jnp.where(below, head, 0.0)
        acc[c, pl.ds(base + frame, ROWS)] += jnp.where(below, 0.0, head)
        acc[c, pl.ds(base + ROWS, frame - ROWS)] += kept(part[ROWS:frame])


def begin_kernel(pos_ref, grads_a, g1_b, acc):
    depth, pos, _ = indices()
    acc[...] = jnp.zeros_like(acc)
    for d, own in ((0, grads_a.at[0]), (1, g1_b)):

        @pl.when(depth == d)
        def _():
            add_window(acc, pos_ref, own, 2 * pos + d, False)


def add_kernel(pos_ref, acc_in, spill_a, acc):
    del acc_in
    depth, pos, left = indices()

    @pl.when(jnp.logical_and(pos > 0, depth != 0))
    def _():
        add_window(acc, pos_ref, spill_a.at[1], 2 * left, True)


def gather_kernel(pos_ref, acc_in, spill_b0, spill_b1, spill_a0, given, out, acc, stage, sems):
    del acc_in
    _, height, frame = acc.shape
    depth, pos, left = indices()
    add_window(acc, pos_ref, given, 2 * pos + 1 - depth, False)

    @pl.when(jnp.logical_and(pos > 0, depth == 0))
    def _():
        add_window(acc, pos_ref, spill_a0, 2 * left, True)
        add_window(acc, pos_ref, spill_b0, 2 * left + 1, True)

    @pl.when(jnp.logical_and(pos > 0, depth != 0))
    def _():
        add_window(acc, pos_ref, spill_b1, 2 * left + 1, True)

    copies = []
    for c in range(2):
        for n, first in enumerate(range(0, height, frame)):
            at = slice(first, first + frame)
            stage[c, at] = acc[c, at].astype(BF)
            copy = pltpu.make_async_copy(stage.at[c, at], out.at[0, c, at], sems.at[c, n])
            copy.start()
            copies.append(copy)
    for copy in copies:
        copy.wait()


def local(n_pos, object_field, probe, prop_phase, measured, positions):
    modes, _, frame, _ = probe.shape
    height = object_field.shape[2]
    both = ("depth", "pos")
    tables = jnp.asarray(split_tables(frame))
    window = jax.ShapeDtypeStruct((2, frame, frame), BF)
    fields = jax.ShapeDtypeStruct((modes, 2, frame, frame), F32)
    vmem = pl.BlockSpec(memory_space=pltpu.VMEM)
    hbm = pl.BlockSpec(memory_space=pltpu.HBM)

    def call(body, name, ins, outs, scratch=(), cost=LIGHT, out_specs=None, aliases=None, vmem_bytes=VMEM_BYTES):
        return pl.pallas_call(
            body,
            name=name,
            in_specs=ins,
            out_specs=jax.tree.map(lambda _: vmem, outs) if out_specs is None else out_specs,
            out_shape=outs,
            input_output_aliases=aliases or {},
            scratch_shapes=scratch,
            compiler_params=pltpu.CompilerParams(vmem_limit_bytes=vmem_bytes),
            cost_estimate=pl.CostEstimate(flops=cost, bytes_accessed=1000, transcendentals=0),
        )

    def dev(d, p):
        return d * n_pos + p

    def leftward(to_of):
        return [(dev(d, p + 1), dev(to, p)) for d, to in to_of for p in range(n_pos - 1)]

    def rightward(to_of):
        return [(dev(d, p), dev(to, p + 1)) for d, to in to_of for p in range(n_pos - 1)]

    positions = positions.T
    def send(name, x, pairs):
        with jax.named_scope(name):
            return lax.ppermute(x, both, pairs)

    swap = [(dev(d, p), dev(1 - d, p)) for d in range(2) for p in range(n_pos)]

    two = jax.ShapeDtypeStruct((2, 2, frame, frame), BF)
    left_a, left_b, mine, pairs = call(
        extract_kernel,
        "extract",
        [vmem, hbm],
        (window, window, window, two),
        [pltpu.VMEM((4, 2, ROWS, frame), BF), pltpu.SemaphoreType.DMA((4, 2))],
        vmem_bytes=EXTRACT_BYTES,
    )(positions, object_field)
    first_a = send("first_a", left_a, leftward([(0, 0)]))
    second_a = send("second_a", left_a, leftward([(1, 0)]))
    swapped = send("swapped", pairs, swap)
    left_b, swapped = lax.optimization_barrier((left_b, swapped))
    first_b = send("first_b", swapped[0], leftward([(1, 1)]))
    second_b = send("second_b", left_b, leftward([(1, 1)]))
    probe_at, kern, measured_at, shift = call(
        functools.partial(prepare_kernel, height),
        "prepare",
        [vmem] * 4,
        (
            jax.ShapeDtypeStruct(probe.shape, BF),
            jax.ShapeDtypeStruct((2, frame, frame), F32),
            jax.ShapeDtypeStruct((frame, frame), F32),
            jax.ShapeDtypeStruct((8, frame), jnp.int32),
        ),
    )(positions, probe, prop_phase, measured)

    packed = [pltpu.VMEM((modes, 2, frame, frame), BF), pltpu.VMEM((modes, frame, 2 * frame), BF)]
    sums_of = jax.ShapeDtypeStruct((modes, 2, frame, frame), BF)
    pair = pltpu.VMEM((2, frame, frame), F32)
    deep = [pair, pltpu.VMEM(fields.shape, F32), pltpu.VMEM((frame, frame), F32), pair] + packed
    def front(core, own, halo):
        body = functools.partial(front_kernel, core)
        return call(body, "front" + "ab"[core], [vmem] * 6, fields, [pair] + packed)(
            shift, own, halo, probe_at, kern, tables
        )

    def tail(core, own, halo, psi):
        body = functools.partial(tail_kernel, core)
        return call(body, "tail" + "ab"[core], [vmem] * 6, (window, sums_of), deep)(
            shift, own, halo, psi, measured_at, tables
        )

    barrier = lax.optimization_barrier
    psi_a = front(0, mine, first_a)
    g1_a, adj_a = tail(0, swapped, second_a, psi_a)
    grads_a = call(back_a_kernel, "backa", [vmem] * 5, two, [pair] + packed)(
        adj_a, g1_a, probe_at, kern, tables
    )
    spill_a = send("spill_a", grads_a, rightward([(0, 1)]))
    first_b, grads_a = barrier((first_b, grads_a))
    psi_b = front(1, swapped, first_b)
    g1_b, adj_b = tail(1, mine, second_b, psi_b)
    give = call(back_b_kernel, "backb", [vmem] * 5, window, [pair] + packed)(
        adj_b, g1_a, probe_at, kern, tables
    )
    spill_b0 = send("spill_b0", give, rightward([(1, 0)]))
    g1_b, give = barrier((g1_b, give))
    spill_b1 = send("spill_b1", g1_b, rightward([(1, 1)]))
    sums = jax.ShapeDtypeStruct((2, height, frame), F32)
    total = call(begin_kernel, "begin", [vmem] * 3, sums, cost=HEAVY)(positions, grads_a, g1_b)
    total, give, spill_a = barrier((total, give, spill_a))
    given = send("given", give, swap)
    spill_a0 = send("spill_a0", spill_a[0], swap)
    total = call(add_kernel, "add", [vmem] * 3, sums, aliases={1: 0}, cost=HEAVY)(
        positions, total, spill_a
    )
    out, _ = call(
        gather_kernel,
        "gather",
        [vmem] * 6,
        (jax.ShapeDtypeStruct(object_field.shape, BF), sums),
        [pltpu.VMEM((2, height, frame), BF), pltpu.SemaphoreType.DMA((2, height // frame))],
        out_specs=(hbm, vmem),
        aliases={1: 1},
    )(positions, total, spill_b0, spill_b1, spill_a0, given)
    return out


def solution(mesh):
    placed = (P("depth", None, None, "pos"), P(), P(), P("pos", None, None), P())
    return jax.shard_map(
        functools.partial(local, mesh.shape["pos"]),
        mesh=mesh,
        in_specs=placed,
        out_specs=P("depth", None, None, "pos"),
        check_vma=False,
    )
```

```python
import functools
import math

import jax
import jax.numpy as jnp
import ml_dtypes
import numpy as np
from jax import lax
from jax.experimental import pallas as pl
from jax.experimental.pallas import tpu as pltpu
from jax.sharding import PartitionSpec as P

BF = jnp.bfloat16
F32 = jnp.float32
ROWS = 16
VMEM_BYTES = 20 << 20
LIGHT, MEDIUM = 1000, 1 << 30
EXTRACT_BYTES = 52 << 20


def split_tables(frame):
    half = frame // 2
    n = np.arange(half)[:, None]
    k = np.arange(half)[None, :]
    factor = 1.0 / math.sqrt(frame)
    mats = []
    for odd in (0, 1):
        angle = (n * (2 * k + odd) % frame) * (2.0 * math.pi / frame)
        re = (np.cos(angle) * factor).astype(ml_dtypes.bfloat16)
        im = (-np.sin(angle) * factor).astype(ml_dtypes.bfloat16)
        mats.append(np.block([[re, im], [-im, re]]))
    return np.stack([mats[0], mats[1], mats[0].T, mats[1].T])


def dot(a, b):
    return jnp.dot(a, b, preferred_element_type=F32)


def load_f32(ref, *index):
    return ref[index].astype(F32)


def store_sums(u, m, lanes, low, high):
    h = low[0].shape[0]
    for c in range(2):
        u[m, 0, c * h : (c + 1) * h, lanes] = (low[c] + high[c]).astype(BF)
        u[m, 1, c * h : (c + 1) * h, lanes] = (low[c] - high[c]).astype(BF)


def rows_fwd(u, v, m, t):
    h = t.shape[-1] // 2
    for k in range(2):
        x = dot(t[2 + k], u[m, k])
        at = pl.ds(k * h, h)
        for c in range(2):
            low, high = x[c * h : (c + 1) * h, :h], x[c * h : (c + 1) * h, h:]
            v[m, at, c * h : (c + 1) * h] = (low + high).astype(BF)
            v[m, at, (2 + c) * h : (3 + c) * h] = (low - high).astype(BF)


def rows_inv(u, v, m, t):
    h = t.shape[-1] // 2
    e, o = dot(t[0], u[m, 0]), dot(t[1], u[m, 1])
    for k, x in enumerate((e + o, e - o)):
        at = pl.ds(k * h, h)
        for c in range(2):
            v[m, at, c * h : (c + 1) * h] = x[c * h : (c + 1) * h, :h].astype(BF)
            v[m, at, (2 + c) * h : (3 + c) * h] = x[c * h : (c + 1) * h, h:].astype(BF)


def cols(v, m, t, inverse, sink):
    h = t.shape[-1] // 2
    k = 2 if inverse else 0
    e, o = dot(v[m, :, : 2 * h], t[k]), dot(v[m, :, 2 * h :], t[k + 1])
    if inverse:
        e, o = e + o, e - o
    for b, x in enumerate((e, o)):
        sink(m, b, (x[:h, :h], x[:h, h:]), (x[h:, :h], x[h:, h:]))


def block(h, a):
    return slice(a * h, (a + 1) * h)


def store_spectrum(u, m, a, b, r, i):
    h = r.shape[0]
    u[m, a, 0:h, block(h, b)] = r.astype(BF)
    u[m, a, h : 2 * h, block(h, b)] = i.astype(BF)


def pick(pos_ref, row, j):
    x = pos_ref[row : row + 1].astype(F32)
    return jnp.sum(jnp.where(columns(x.shape) == j, x, 0.0)).astype(jnp.int32)


def place(pos_ref, j, height, frame):
    y = pick(pos_ref, 0, j)
    base = jnp.minimum((y >> 4) << 4, height - frame - ROWS)
    return pl.multiple_of(base, ROWS), y - base, pick(pos_ref, 1, j) & (frame - 1)


def indices():
    depth, pos = lax.axis_index("depth"), lax.axis_index("pos")
    left = jnp.maximum(pos - 1, 0)
    return depth, pos, left


def columns(shape):
    return lax.broadcasted_iota(jnp.int32, shape, len(shape) - 1)


def rows(shape):
    return lax.broadcasted_iota(jnp.int32, shape, len(shape) - 2)


def extract_kernel(pos_ref, obj_ref, left_a, left_b, mine, pair, ends, sems):
    _, _, height, frame = obj_ref.shape
    depth, pos, left = indices()
    src = obj_ref.at[0]
    jobs = []
    for w, (outs, j) in enumerate(
        [
            ((left_a,), 2 * left),
            ((left_b, pair.at[0]), 2 * left + 1),
            ((pair.at[1],), 2 * pos + 1 - depth),
            ((mine,), 2 * pos + depth),
        ]
    ):
        base, shift, _ = place(pos_ref, j, height, frame)
        body = pltpu.make_async_copy(src.at[:, pl.ds(base, frame)], outs[0], sems.at[w, 0])
        end = pltpu.make_async_copy(src.at[:, pl.ds(base + frame, ROWS)], ends.at[w], sems.at[w, 1])
        end.start()
        body.start()
        jobs.append((outs, body, end, shift))
    for w, (outs, body, end, shift) in enumerate(jobs):
        end.wait()
        body.wait()
        upper, lower = outs[0][:, 0:ROWS].astype(F32), ends[w].astype(F32)
        outs[0][:, 0:ROWS] = jnp.where(rows(upper.shape) >= shift, upper, lower).astype(BF)
        for copy in outs[1:]:
            copy[...] = outs[0][...]


def cos_sin(x):
    x = x - jnp.floor(x * (0.5 / math.pi) + 0.5) * (2.0 * math.pi)
    t = 0.5 * x
    z = t * t
    sine = t * (1.0 + z * (-1 / 6 + z * (1 / 120 + z * (-1 / 5040 + z * (1 / 362880 - z / 39916800)))))
    cosine = 1.0 + z * (
        -1 / 2 + z * (1 / 24 + z * (-1 / 720 + z * (1 / 40320 + z * (-1 / 3628800 + z / 479001600))))
    )
    return 1.0 - 2.0 * sine * sine, 2.0 * sine * cosine


def prepare_kernel(height, pos_ref, probe_ref, phase_ref, measured_ref, probe_out, kern_out, measured_out, shift_out):
    modes, _, frame, _ = probe_ref.shape
    depth, pos, _ = indices()
    half = frame // 2
    _, row_shift, col_shift = place(pos_ref, 2 * pos + depth, height, frame)
    shift_out[...] = jnp.full(shift_out.shape, col_shift, jnp.int32)
    down = lax.broadcasted_iota(jnp.int32, (frame, frame), 0)
    across = lax.broadcasted_iota(jnp.int32, (frame, frame), 1)

    def chosen(where):
        return jnp.where(where, 1.0, 0.0).astype(BF)

    def even_odd(n):
        return jnp.where(n < half, 2 * n, 2 * (n - half) + 1)

    order, order_t = chosen(across == even_odd(down)), chosen(down == even_odd(across))
    turn = chosen(across == ((down - row_shift) & (frame - 1)))

    def reorder(x):
        for axis in (0, 1):
            high = x.astype(BF)
            low = (x - high.astype(F32)).astype(BF)
            if axis == 0:
                x = dot(order, high) + dot(order, low)
            else:
                x = dot(high, order_t) + dot(low, order_t)
        return x

    kern_out[0], kern_out[1] = cos_sin(reorder(phase_ref[...]))
    for m in range(modes):
        for c in range(2):
            plane = pltpu.roll(probe_ref[m, c].astype(F32), col_shift, 1).astype(BF)
            probe_out[m, c] = dot(turn, plane).astype(BF)
    measured_out[...] = reorder(measured_ref[depth])


def join(shift, obj, own, halo):
    for c in range(2):
        near = own[c].astype(F32)
        obj[c] = jnp.where(columns(near.shape) >= shift[0:1], near, halo[c].astype(F32))


def front_steps(obj, probe, kern, t, psi, u, v):
    h = t.shape[-1] // 2
    modes = range(probe.shape[0])
    for m in modes:
        halves = []
        for a in range(2):
            at = block(h, a)
            pr, pi = load_f32(probe, m, 0, at), load_f32(probe, m, 1, at)
            qr, qi = obj[0, at], obj[1, at]
            halves.append((pr * qr - pi * qi, pr * qi + pi * qr))
        store_sums(u, m, slice(None), *halves)
    for m in modes:
        rows_fwd(u, v, m, t)

    def spectrum(m, b, *halves):
        for a, (r, i) in enumerate(halves):
            kr, ki = kern[0, block(h, a), block(h, b)], kern[1, block(h, a), block(h, b)]
            store_spectrum(u, m, a, b, r * kr - i * ki, r * ki + i * kr)

    def wave(m, b, *halves):
        for a, (r, i) in enumerate(halves):
            psi[m, 0, block(h, a), block(h, b)] = r
            psi[m, 1, block(h, a), block(h, b)] = i

    for m in modes:
        cols(v, m, t, False, spectrum)
    for m in modes:
        rows_inv(u, v, m, t)
    for m in modes:
        cols(v, m, t, True, wave)


def tail_steps(obj, psi, measured, t, g1, adj, far, inten, total, u, v):
    h = t.shape[-1] // 2
    modes = range(psi.shape[0])
    for m in modes:
        halves = []
        for a in range(2):
            at = block(h, a)
            pr, pi, qr, qi = psi[m, 0, at], psi[m, 1, at], obj[0, at], obj[1, at]
            halves.append((pr * qr - pi * qi, pr * qi + pi * qr))
        store_sums(u, m, slice(None), *halves)
    for m in modes:
        rows_fwd(u, v, m, t)

    def detect(m, b, *halves):
        for a, (r, i) in enumerate(halves):
            at = (block(h, a), block(h, b))
            far[(m, 0) + at] = r
            far[(m, 1) + at] = i
            power = r * r + i * i
            inten[at] = power if m == 0 else inten[at] + power

    for m in modes:
        cols(v, m, t, False, detect)
    for a in range(2):
        for b in range(2):
            at = (block(h, a), block(h, b))
            weight = (inten[at] - measured[at].astype(F32)) * 0.125
            for m in modes:
                store_spectrum(u, m, a, b, weight * far[(m, 0) + at], weight * far[(m, 1) + at])
    for m in modes:
        rows_inv(u, v, m, t)
    last = psi.shape[0] - 1

    def back(m, b, *halves):
        adjoint = []
        for a, (r, i) in enumerate(halves):
            at = (block(h, a), block(h, b))
            pr, pi = psi[(m, 0) + at], psi[(m, 1) + at]
            add_up(g1, total, at, m == 0, m == last, pr * r + pi * i, pr * i - pi * r)
            qr, qi = obj[(0,) + at], obj[(1,) + at]
            adjoint.append((qr * r + qi * i, qr * i - qi * r))
        store_sums(adj, m, block(h, b), *adjoint)

    for m in modes:
        cols(v, m, t, True, back)


def back_steps(adj, probe, kern, t, g0, total, u, v):
    h = t.shape[-1] // 2
    modes = range(probe.shape[0])
    for m in modes:
        rows_fwd(adj, v, m, t)

    def spectrum(m, b, *halves):
        for a, (r, i) in enumerate(halves):
            kr, ki = kern[0, block(h, a), block(h, b)], kern[1, block(h, a), block(h, b)]
            store_spectrum(u, m, a, b, kr * r + ki * i, kr * i - ki * r)

    for m in modes:
        cols(v, m, t, False, spectrum)
    for m in modes:
        rows_inv(u, v, m, t)
    last = probe.shape[0] - 1

    def back(m, b, *halves):
        for a, (r, i) in enumerate(halves):
            at = (block(h, a), block(h, b))
            pr, pi = load_f32(probe, m, 0, *at), load_f32(probe, m, 1, *at)
            add_up(g0, total, at, m == 0, m == last, pr * r + pi * i, pr * i - pi * r)

    for m in modes:
        cols(v, m, t, True, back)


def add_up(out, total, at, first, last, *parts):
    for c, part in enumerate(parts):
        if not first:
            part = part + total[(c,) + at]
        if last:
            out[(c,) + at] = part.astype(BF)
        else:
            total[(c,) + at] = part


def front_kernel(core, shift, own, halo, probe, kern, t, psi, obj, u, v):
    @pl.when(lax.axis_index("depth") == core)
    def _():
        join(shift, obj, own if core == 0 else own.at[1], halo)
        front_steps(obj, probe, kern, t, psi, u, v)


def tail_kernel(core, shift, own, halo, psi, measured, t, g1, adj, obj, far, inten, total, u, v):
    @pl.when(lax.axis_index("depth") == core)
    def _():
        join(shift, obj, own if core == 1 else own.at[1], halo)
        tail_steps(obj, psi, measured, t, g1, adj, far, inten, total, u, v)


def back_a_kernel(adj, probe, kern, t, g0, total, u, v):
    @pl.when(lax.axis_index("depth") == 0)
    def _():
        back_steps(adj, probe, kern, t, g0, total, u, v)


def back_b_kernel(adj, g1_a, probe, kern, t, give, total, u, v):
    depth, _, _ = indices()

    @pl.when(depth == 0)
    def _():
        give[...] = g1_a[...]

    @pl.when(depth != 0)
    def _():
        back_steps(adj, probe, kern, t, give, total, u, v)


def add_window(acc, pos_ref, piece, j, spill):
    _, height, frame = acc.shape
    base, row_shift, col_shift = place(pos_ref, j, height, frame)

    def kept(x):
        keep = columns(x.shape) < col_shift if spill else columns(x.shape) >= col_shift
        return jnp.where(keep, x.astype(F32), 0.0)

    for c in range(2):
        part = piece[c] if isinstance(piece, tuple) else piece.at[c]
        head = kept(part[0:ROWS])
        below = rows(head.shape) >= row_shift
        acc[c, pl.ds(base, ROWS)] += jnp.where(below, head, 0.0)
        acc[c, pl.ds(base + frame, ROWS)] += jnp.where(below, 0.0, head)
        acc[c, pl.ds(base + ROWS, frame - ROWS)] += kept(part[ROWS:frame])


def begin_kernel(pos_ref, g0_a, g1_b, acc):
    depth, pos, _ = indices()
    acc[...] = jnp.zeros_like(acc)
    for d, own in ((0, g0_a), (1, g1_b)):

        @pl.when(depth == d)
        def _():
            add_window(acc, pos_ref, own, 2 * pos + d, False)


def trade_kernel(spill_b1, spill_a0, out):
    for d, spill in ((0, spill_b1), (1, spill_a0)):

        @pl.when(lax.axis_index("depth") == d)
        def _():
            out[...] = spill[...]


def add_kernel(pos_ref, acc_in, spill_a1, acc):
    del acc_in
    depth, pos, left = indices()

    @pl.when(jnp.logical_and(pos > 0, depth != 0))
    def _():
        add_window(acc, pos_ref, spill_a1, 2 * left, True)


def gather_kernel(pos_ref, acc_in, spill_b0, traded, given, out, acc, stage, sems):
    del acc_in
    _, height, frame = acc.shape
    depth, pos, left = indices()
    add_window(acc, pos_ref, given, 2 * pos + 1 - depth, False)

    @pl.when(pos > 0)
    def _():
        add_window(acc, pos_ref, traded, 2 * left + depth, True)

    @pl.when(jnp.logical_and(pos > 0, depth == 0))
    def _():
        add_window(acc, pos_ref, spill_b0, 2 * left + 1, True)

    copies = []
    for c in range(2):
        for n, first in enumerate(range(0, height, frame)):
            at = slice(first, first + frame)
            stage[c, at] = acc[c, at].astype(BF)
            copy = pltpu.make_async_copy(stage.at[c, at], out.at[0, c, at], sems.at[c, n])
            copy.start()
            copies.append(copy)
    for copy in copies:
        copy.wait()


def local(n_pos, object_field, probe, prop_phase, measured, positions):
    modes, _, frame, _ = probe.shape
    height = object_field.shape[2]
    both = ("depth", "pos")
    tables = jnp.asarray(split_tables(frame))
    window = jax.ShapeDtypeStruct((2, frame, frame), BF)
    fields = jax.ShapeDtypeStruct((modes, 2, frame, frame), F32)
    vmem = pl.BlockSpec(memory_space=pltpu.VMEM)
    hbm = pl.BlockSpec(memory_space=pltpu.HBM)

    def call(body, name, ins, outs, scratch=(), cost=LIGHT, out_specs=None, aliases=None, vmem_bytes=VMEM_BYTES):
        return pl.pallas_call(
            body,
            name=name,
            in_specs=ins,
            out_specs=jax.tree.map(lambda _: vmem, outs) if out_specs is None else out_specs,
            out_shape=outs,
            input_output_aliases=aliases or {},
            scratch_shapes=scratch,
            compiler_params=pltpu.CompilerParams(vmem_limit_bytes=vmem_bytes),
            cost_estimate=pl.CostEstimate(flops=cost, bytes_accessed=1000, transcendentals=0),
        )

    def dev(d, p):
        return d * n_pos + p

    def leftward(to_of):
        return [(dev(d, p + 1), dev(to, p)) for d, to in to_of for p in range(n_pos - 1)]

    def rightward(to_of):
        return [(dev(d, p), dev(to, p + 1)) for d, to in to_of for p in range(n_pos - 1)]

    positions = positions.T
    def send(name, x, pairs):
        with jax.named_scope(name):
            return lax.ppermute(x, both, pairs)

    swap = [(dev(d, p), dev(1 - d, p)) for d in range(2) for p in range(n_pos)]

    two = jax.ShapeDtypeStruct((2, 2, frame, frame), BF)
    left_a, left_b, mine, pairs = call(
        extract_kernel,
        "extract",
        [vmem, hbm],
        (window, window, window, two),
        [pltpu.VMEM((4, 2, ROWS, frame), BF), pltpu.SemaphoreType.DMA((4, 2))],
        vmem_bytes=EXTRACT_BYTES,
    )(positions, object_field)
    first_a = send("first_a", left_a, leftward([(0, 0)]))
    second_a = send("second_a", left_a, leftward([(1, 0)]))
    swapped = send("swapped", pairs, swap)
    left_b, swapped = lax.optimization_barrier((left_b, swapped))
    first_b = send("first_b", swapped[0], leftward([(1, 1)]))
    second_b = send("second_b", left_b, leftward([(1, 1)]))
    probe_at, kern, measured_at, shift = call(
        functools.partial(prepare_kernel, height),
        "prepare",
        [vmem] * 4,
        (
            jax.ShapeDtypeStruct(probe.shape, BF),
            jax.ShapeDtypeStruct((2, frame, frame), F32),
            jax.ShapeDtypeStruct((frame, frame), F32),
            jax.ShapeDtypeStruct((8, frame), jnp.int32),
        ),
    )(positions, probe, prop_phase, measured)

    packed = [pltpu.VMEM((modes, 2, frame, frame), BF), pltpu.VMEM((modes, frame, 2 * frame), BF)]
    sums_of = jax.ShapeDtypeStruct((modes, 2, frame, frame), BF)
    pair = pltpu.VMEM((2, frame, frame), F32)
    deep = [pair, pltpu.VMEM(fields.shape, F32), pltpu.VMEM((frame, frame), F32), pair] + packed
    def front(core, own, halo):
        body = functools.partial(front_kernel, core)
        return call(body, "front" + "ab"[core], [vmem] * 6, fields, [pair] + packed)(
            shift, own, halo, probe_at, kern, tables
        )

    def tail(core, own, halo, psi):
        body = functools.partial(tail_kernel, core)
        return call(body, "tail" + "ab"[core], [vmem] * 6, (window, sums_of), deep)(
            shift, own, halo, psi, measured_at, tables
        )

    barrier = lax.optimization_barrier
    psi_a = front(0, mine, first_a)
    g1_a, adj_a = tail(0, swapped, second_a, psi_a)
    spill_a1 = send("spill_a1", g1_a, rightward([(0, 1)]))
    g0_a = call(back_a_kernel, "backa", [vmem] * 4, window, [pair] + packed)(
        adj_a, probe_at, kern, tables
    )
    spill_a0 = send("spill_a0", g0_a, rightward([(0, 1)]))
    first_b, g0_a = barrier((first_b, g0_a))
    psi_b = front(1, swapped, first_b)
    g1_b, adj_b = tail(1, mine, second_b, psi_b)
    spill_b1 = send("spill_b1", g1_b, rightward([(1, 0)]))
    give = call(back_b_kernel, "backb", [vmem] * 5, window, [pair] + packed)(
        adj_b, g1_a, probe_at, kern, tables
    )
    spill_b0 = send("spill_b0", give, rightward([(1, 0)]))
    sums = jax.ShapeDtypeStruct((2, height, frame), F32)
    total = call(begin_kernel, "begin", [vmem] * 3, sums)(positions, g0_a, g1_b)
    total, give, spill_a1 = barrier((total, give, spill_a1))
    total = call(add_kernel, "add", [vmem] * 3, sums, aliases={1: 0}, cost=MEDIUM)(
        positions, total, spill_a1
    )
    total, give, spill_b1, spill_a0 = barrier((total, give, spill_b1, spill_a0))
    given = send("given", give, swap)
    trade = call(trade_kernel, "trade", [vmem] * 2, window)(spill_b1, spill_a0)
    traded = send("traded", trade, swap)
    out, _ = call(
        gather_kernel,
        "gather",
        [vmem] * 5,
        (jax.ShapeDtypeStruct(object_field.shape, BF), sums),
        [pltpu.VMEM((2, height, frame), BF), pltpu.SemaphoreType.DMA((2, height // frame))],
        out_specs=(hbm, vmem),
        aliases={1: 1},
    )(positions, total, spill_b0, traded, given)
    return out


def solution(mesh):
    placed = (P("depth", None, None, "pos"), P(), P(), P("pos", None, None), P())
    return jax.shard_map(
        functools.partial(local, mesh.shape["pos"]),
        mesh=mesh,
        in_specs=placed,
        out_specs=P("depth", None, None, "pos"),
        check_vma=False,
    )
```

```python
import functools
import math

import jax
import jax.numpy as jnp
import ml_dtypes
import numpy as np
from jax import lax
from jax.experimental import pallas as pl
from jax.experimental.pallas import tpu as pltpu
from jax.sharding import PartitionSpec as P

BF = jnp.bfloat16
F32 = jnp.float32
ROWS = 16
VMEM_BYTES = 20 << 20
LIGHT, MEDIUM = 1000, 1 << 30
EXTRACT_BYTES = 52 << 20


def split_tables(frame):
    half = frame // 2
    n = np.arange(half)[:, None]
    k = np.arange(half)[None, :]
    factor = 1.0 / math.sqrt(frame)
    mats = []
    for odd in (0, 1):
        angle = (n * (2 * k + odd) % frame) * (2.0 * math.pi / frame)
        re = (np.cos(angle) * factor).astype(ml_dtypes.bfloat16)
        im = (-np.sin(angle) * factor).astype(ml_dtypes.bfloat16)
        mats.append(np.block([[re, im], [-im, re]]))
    return np.stack([mats[0], mats[1], mats[0].T, mats[1].T])


def dot(a, b):
    return jnp.dot(a, b, preferred_element_type=F32)


def load_f32(ref, *index):
    return ref[index].astype(F32)


def store_sums(u, m, lanes, low, high):
    h = low[0].shape[0]
    for c in range(2):
        u[m, 0, c * h : (c + 1) * h, lanes] = (low[c] + high[c]).astype(BF)
        u[m, 1, c * h : (c + 1) * h, lanes] = (low[c] - high[c]).astype(BF)


def rows_fwd(u, v, m, t):
    h = t.shape[-1] // 2
    for k in range(2):
        x = dot(t[2 + k], u[m, k])
        at = pl.ds(k * h, h)
        for c in range(2):
            low, high = x[c * h : (c + 1) * h, :h], x[c * h : (c + 1) * h, h:]
            v[m, at, c * h : (c + 1) * h] = (low + high).astype(BF)
            v[m, at, (2 + c) * h : (3 + c) * h] = (low - high).astype(BF)


def rows_inv(u, v, m, t):
    h = t.shape[-1] // 2
    e, o = dot(t[0], u[m, 0]), dot(t[1], u[m, 1])
    for k, x in enumerate((e + o, e - o)):
        at = pl.ds(k * h, h)
        for c in range(2):
            v[m, at, c * h : (c + 1) * h] = x[c * h : (c + 1) * h, :h].astype(BF)
            v[m, at, (2 + c) * h : (3 + c) * h] = x[c * h : (c + 1) * h, h:].astype(BF)


def cols(v, m, t, inverse, sink):
    h = t.shape[-1] // 2
    k = 2 if inverse else 0
    e, o = dot(v[m, :, : 2 * h], t[k]), dot(v[m, :, 2 * h :], t[k + 1])
    if inverse:
        e, o = e + o, e - o
    for b, x in enumerate((e, o)):
        sink(m, b, (x[:h, :h], x[:h, h:]), (x[h:, :h], x[h:, h:]))


def block(h, a):
    return slice(a * h, (a + 1) * h)


def store_spectrum(u, m, a, b, r, i):
    h = r.shape[0]
    u[m, a, 0:h, block(h, b)] = r.astype(BF)
    u[m, a, h : 2 * h, block(h, b)] = i.astype(BF)


def pick(pos_ref, row, j):
    x = pos_ref[row : row + 1].astype(F32)
    return jnp.sum(jnp.where(columns(x.shape) == j, x, 0.0)).astype(jnp.int32)


def place(pos_ref, j, height, frame):
    y = pick(pos_ref, 0, j)
    base = jnp.minimum((y >> 4) << 4, height - frame - ROWS)
    return pl.multiple_of(base, ROWS), y - base, pick(pos_ref, 1, j) & (frame - 1)


def indices():
    depth, pos = lax.axis_index("depth"), lax.axis_index("pos")
    left = jnp.maximum(pos - 1, 0)
    return depth, pos, left


def columns(shape):
    return lax.broadcasted_iota(jnp.int32, shape, len(shape) - 1)


def rows(shape):
    return lax.broadcasted_iota(jnp.int32, shape, len(shape) - 2)


def extract_kernel(pos_ref, obj_ref, left_a, left_b, mine, pair, ends, sems):
    _, _, height, frame = obj_ref.shape
    depth, pos, left = indices()
    src = obj_ref.at[0]
    jobs = []
    for w, (outs, j) in enumerate(
        [
            ((left_a,), 2 * left),
            ((left_b, pair.at[0]), 2 * left + 1),
            ((pair.at[1],), 2 * pos + 1 - depth),
            ((mine,), 2 * pos + depth),
        ]
    ):
        base, shift, _ = place(pos_ref, j, height, frame)
        body = pltpu.make_async_copy(src.at[:, pl.ds(base, frame)], outs[0], sems.at[w, 0])
        end = pltpu.make_async_copy(src.at[:, pl.ds(base + frame, ROWS)], ends.at[w], sems.at[w, 1])
        end.start()
        body.start()
        jobs.append((outs, body, end, shift))
    for w, (outs, body, end, shift) in enumerate(jobs):
        end.wait()
        body.wait()
        upper, lower = outs[0][:, 0:ROWS].astype(F32), ends[w].astype(F32)
        outs[0][:, 0:ROWS] = jnp.where(rows(upper.shape) >= shift, upper, lower).astype(BF)
        for copy in outs[1:]:
            copy[...] = outs[0][...]


def cos_sin(x):
    x = x - jnp.floor(x * (0.5 / math.pi) + 0.5) * (2.0 * math.pi)
    t = 0.5 * x
    z = t * t
    sine = t * (1.0 + z * (-1 / 6 + z * (1 / 120 + z * (-1 / 5040 + z * (1 / 362880 - z / 39916800)))))
    cosine = 1.0 + z * (
        -1 / 2 + z * (1 / 24 + z * (-1 / 720 + z * (1 / 40320 + z * (-1 / 3628800 + z / 479001600))))
    )
    return 1.0 - 2.0 * sine * sine, 2.0 * sine * cosine


def prepare_steps(
    core, height, pos_ref, probe_ref, phase_ref, measured_ref, probe_out, kern_out, measured_out, shift_out
):
    modes, _, frame, _ = probe_ref.shape
    _, pos, _ = indices()
    half = frame // 2
    _, row_shift, col_shift = place(pos_ref, 2 * pos + core, height, frame)
    shift_out[...] = jnp.full(shift_out.shape, col_shift, jnp.int32)
    down = lax.broadcasted_iota(jnp.int32, (frame, frame), 0)
    across = lax.broadcasted_iota(jnp.int32, (frame, frame), 1)

    def chosen(where):
        return jnp.where(where, 1.0, 0.0).astype(BF)

    def even_odd(n):
        return jnp.where(n < half, 2 * n, 2 * (n - half) + 1)

    order, order_t = chosen(across == even_odd(down)), chosen(down == even_odd(across))
    turn = chosen(across == ((down - row_shift) & (frame - 1)))

    def reorder(x):
        for axis in (0, 1):
            high = x.astype(BF)
            low = (x - high.astype(F32)).astype(BF)
            if axis == 0:
                x = dot(order, high) + dot(order, low)
            else:
                x = dot(high, order_t) + dot(low, order_t)
        return x

    kern_out[0], kern_out[1] = cos_sin(reorder(phase_ref[...]))
    for m in range(modes):
        for c in range(2):
            plane = pltpu.roll(probe_ref[m, c].astype(F32), col_shift, 1).astype(BF)
            probe_out[m, c] = dot(turn, plane).astype(BF)
    measured_out[...] = reorder(measured_ref[core])


def prepare_kernel(core, *rest):
    @pl.when(lax.axis_index("depth") == core)
    def _():
        prepare_steps(core, *rest)


def join(shift, obj, own, halo):
    for c in range(2):
        near = own[c].astype(F32)
        obj[c] = jnp.where(columns(near.shape) >= shift[0:1], near, halo[c].astype(F32))


def front_steps(obj, probe, kern, t, psi, u, v):
    h = t.shape[-1] // 2
    modes = range(probe.shape[0])
    for m in modes:
        halves = []
        for a in range(2):
            at = block(h, a)
            pr, pi = load_f32(probe, m, 0, at), load_f32(probe, m, 1, at)
            qr, qi = obj[0, at], obj[1, at]
            halves.append((pr * qr - pi * qi, pr * qi + pi * qr))
        store_sums(u, m, slice(None), *halves)
    for m in modes:
        rows_fwd(u, v, m, t)

    def spectrum(m, b, *halves):
        for a, (r, i) in enumerate(halves):
            kr, ki = kern[0, block(h, a), block(h, b)], kern[1, block(h, a), block(h, b)]
            store_spectrum(u, m, a, b, r * kr - i * ki, r * ki + i * kr)

    def wave(m, b, *halves):
        for a, (r, i) in enumerate(halves):
            psi[m, 0, block(h, a), block(h, b)] = r
            psi[m, 1, block(h, a), block(h, b)] = i

    for m in modes:
        cols(v, m, t, False, spectrum)
    for m in modes:
        rows_inv(u, v, m, t)
    for m in modes:
        cols(v, m, t, True, wave)


def tail_steps(obj, psi, measured, t, g1, adj, far, inten, total, u, v):
    h = t.shape[-1] // 2
    modes = range(psi.shape[0])
    for m in modes:
        halves = []
        for a in range(2):
            at = block(h, a)
            pr, pi, qr, qi = psi[m, 0, at], psi[m, 1, at], obj[0, at], obj[1, at]
            halves.append((pr * qr - pi * qi, pr * qi + pi * qr))
        store_sums(u, m, slice(None), *halves)
    for m in modes:
        rows_fwd(u, v, m, t)

    def detect(m, b, *halves):
        for a, (r, i) in enumerate(halves):
            at = (block(h, a), block(h, b))
            far[(m, 0) + at] = r
            far[(m, 1) + at] = i
            power = r * r + i * i
            inten[at] = power if m == 0 else inten[at] + power

    for m in modes:
        cols(v, m, t, False, detect)
    for a in range(2):
        for b in range(2):
            at = (block(h, a), block(h, b))
            weight = (inten[at] - measured[at].astype(F32)) * 0.125
            for m in modes:
                store_spectrum(u, m, a, b, weight * far[(m, 0) + at], weight * far[(m, 1) + at])
    for m in modes:
        rows_inv(u, v, m, t)
    last = psi.shape[0] - 1

    def back(m, b, *halves):
        adjoint = []
        for a, (r, i) in enumerate(halves):
            at = (block(h, a), block(h, b))
            pr, pi = psi[(m, 0) + at], psi[(m, 1) + at]
            add_up(g1, total, at, m == 0, m == last, pr * r + pi * i, pr * i - pi * r)
            qr, qi = obj[(0,) + at], obj[(1,) + at]
            adjoint.append((qr * r + qi * i, qr * i - qi * r))
        store_sums(adj, m, block(h, b), *adjoint)

    for m in modes:
        cols(v, m, t, True, back)


def back_steps(adj, probe, kern, t, g0, total, u, v):
    h = t.shape[-1] // 2
    modes = range(probe.shape[0])
    for m in modes:
        rows_fwd(adj, v, m, t)

    def spectrum(m, b, *halves):
        for a, (r, i) in enumerate(halves):
            kr, ki = kern[0, block(h, a), block(h, b)], kern[1, block(h, a), block(h, b)]
            store_spectrum(u, m, a, b, kr * r + ki * i, kr * i - ki * r)

    for m in modes:
        cols(v, m, t, False, spectrum)
    for m in modes:
        rows_inv(u, v, m, t)
    last = probe.shape[0] - 1

    def back(m, b, *halves):
        for a, (r, i) in enumerate(halves):
            at = (block(h, a), block(h, b))
            pr, pi = load_f32(probe, m, 0, *at), load_f32(probe, m, 1, *at)
            add_up(g0, total, at, m == 0, m == last, pr * r + pi * i, pr * i - pi * r)

    for m in modes:
        cols(v, m, t, True, back)


def add_up(out, total, at, first, last, *parts):
    for c, part in enumerate(parts):
        if not first:
            part = part + total[(c,) + at]
        if last:
            out[(c,) + at] = part.astype(BF)
        else:
            total[(c,) + at] = part


def front_kernel(core, shift, own, halo, probe, kern, t, psi, obj, u, v):
    @pl.when(lax.axis_index("depth") == core)
    def _():
        join(shift, obj, own if core == 0 else own.at[1], halo)
        front_steps(obj, probe, kern, t, psi, u, v)


def tail_kernel(core, shift, own, halo, psi, measured, t, g1, adj, obj, far, inten, total, u, v):
    @pl.when(lax.axis_index("depth") == core)
    def _():
        join(shift, obj, own if core == 1 else own.at[1], halo)
        tail_steps(obj, psi, measured, t, g1, adj, far, inten, total, u, v)


def back_a_kernel(adj, probe, kern, t, g0, total, u, v):
    @pl.when(lax.axis_index("depth") == 0)
    def _():
        back_steps(adj, probe, kern, t, g0, total, u, v)


def back_b_kernel(adj, g1_a, probe, kern, t, give, total, u, v):
    depth, _, _ = indices()

    @pl.when(depth == 0)
    def _():
        give[...] = g1_a[...]

    @pl.when(depth != 0)
    def _():
        back_steps(adj, probe, kern, t, give, total, u, v)


def add_window(acc, pos_ref, piece, j, spill):
    _, height, frame = acc.shape
    base, row_shift, col_shift = place(pos_ref, j, height, frame)

    def kept(x):
        keep = columns(x.shape) < col_shift if spill else columns(x.shape) >= col_shift
        return jnp.where(keep, x.astype(F32), 0.0)

    for c in range(2):
        part = piece[c] if isinstance(piece, tuple) else piece.at[c]
        head = kept(part[0:ROWS])
        below = rows(head.shape) >= row_shift
        acc[c, pl.ds(base, ROWS)] += jnp.where(below, head, 0.0)
        acc[c, pl.ds(base + frame, ROWS)] += jnp.where(below, 0.0, head)
        acc[c, pl.ds(base + ROWS, frame - ROWS)] += kept(part[ROWS:frame])


def begin_kernel(pos_ref, g0_a, g1_b, acc):
    depth, pos, _ = indices()
    acc[...] = jnp.zeros_like(acc)
    for d, own in ((0, g0_a), (1, g1_b)):

        @pl.when(depth == d)
        def _():
            add_window(acc, pos_ref, own, 2 * pos + d, False)


def trade_kernel(spill_b1, spill_a0, out):
    for d, spill in ((0, spill_b1), (1, spill_a0)):

        @pl.when(lax.axis_index("depth") == d)
        def _():
            out[...] = spill[...]


def add_kernel(pos_ref, acc_in, spill_a1, acc):
    del acc_in
    depth, pos, left = indices()

    @pl.when(jnp.logical_and(pos > 0, depth != 0))
    def _():
        add_window(acc, pos_ref, spill_a1, 2 * left, True)


def gather_kernel(pos_ref, acc_in, spill_b0, traded, given, out, acc, stage, sems):
    del acc_in
    _, height, frame = acc.shape
    depth, pos, left = indices()
    add_window(acc, pos_ref, given, 2 * pos + 1 - depth, False)

    @pl.when(pos > 0)
    def _():
        add_window(acc, pos_ref, traded, 2 * left + depth, True)

    @pl.when(jnp.logical_and(pos > 0, depth == 0))
    def _():
        add_window(acc, pos_ref, spill_b0, 2 * left + 1, True)

    copies = []
    for c in range(2):
        for n, first in enumerate(range(0, height, frame)):
            at = slice(first, first + frame)
            stage[c, at] = acc[c, at].astype(BF)
            copy = pltpu.make_async_copy(stage.at[c, at], out.at[0, c, at], sems.at[c, n])
            copy.start()
            copies.append(copy)
    for copy in copies:
        copy.wait()


def local(n_pos, object_field, probe, prop_phase, measured, positions):
    modes, _, frame, _ = probe.shape
    height = object_field.shape[2]
    both = ("depth", "pos")
    tables = jnp.asarray(split_tables(frame))
    window = jax.ShapeDtypeStruct((2, frame, frame), BF)
    fields = jax.ShapeDtypeStruct((modes, 2, frame, frame), F32)
    vmem = pl.BlockSpec(memory_space=pltpu.VMEM)
    hbm = pl.BlockSpec(memory_space=pltpu.HBM)

    def call(body, name, ins, outs, scratch=(), cost=LIGHT, out_specs=None, aliases=None, vmem_bytes=VMEM_BYTES):
        return pl.pallas_call(
            body,
            name=name,
            in_specs=ins,
            out_specs=jax.tree.map(lambda _: vmem, outs) if out_specs is None else out_specs,
            out_shape=outs,
            input_output_aliases=aliases or {},
            scratch_shapes=scratch,
            compiler_params=pltpu.CompilerParams(vmem_limit_bytes=vmem_bytes),
            cost_estimate=pl.CostEstimate(flops=cost, bytes_accessed=1000, transcendentals=0),
        )

    def dev(d, p):
        return d * n_pos + p

    def leftward(to_of):
        return [(dev(d, p + 1), dev(to, p)) for d, to in to_of for p in range(n_pos - 1)]

    def rightward(to_of):
        return [(dev(d, p), dev(to, p + 1)) for d, to in to_of for p in range(n_pos - 1)]

    positions = positions.T
    def send(name, x, pairs):
        with jax.named_scope(name):
            return lax.ppermute(x, both, pairs)

    swap = [(dev(d, p), dev(1 - d, p)) for d in range(2) for p in range(n_pos)]

    two = jax.ShapeDtypeStruct((2, 2, frame, frame), BF)
    left_a, left_b, mine, pairs = call(
        extract_kernel,
        "extract",
        [vmem, hbm],
        (window, window, window, two),
        [pltpu.VMEM((4, 2, ROWS, frame), BF), pltpu.SemaphoreType.DMA((4, 2))],
        vmem_bytes=EXTRACT_BYTES,
    )(positions, object_field)
    first_a = send("first_a", left_a, leftward([(0, 0)]))
    second_a = send("second_a", left_a, leftward([(1, 0)]))
    swapped = send("swapped", pairs, swap)
    left_b, swapped = lax.optimization_barrier((left_b, swapped))
    first_b = send("first_b", swapped[0], leftward([(1, 1)]))
    second_b = send("second_b", left_b, leftward([(1, 1)]))
    def prepare(core):
        return call(
            functools.partial(prepare_kernel, core, height),
            "prepare" + "ab"[core],
            [vmem] * 4,
            (
                jax.ShapeDtypeStruct(probe.shape, BF),
                jax.ShapeDtypeStruct((2, frame, frame), F32),
                jax.ShapeDtypeStruct((frame, frame), F32),
                jax.ShapeDtypeStruct((8, frame), jnp.int32),
            ),
        )(positions, probe, prop_phase, measured)

    packed = [pltpu.VMEM((modes, 2, frame, frame), BF), pltpu.VMEM((modes, frame, 2 * frame), BF)]
    sums_of = jax.ShapeDtypeStruct((modes, 2, frame, frame), BF)
    pair = pltpu.VMEM((2, frame, frame), F32)
    deep = [pair, pltpu.VMEM(fields.shape, F32), pltpu.VMEM((frame, frame), F32), pair] + packed
    def front(core, own, halo):
        body = functools.partial(front_kernel, core)
        probe_at, kern, _, shift = ready[core]
        return call(body, "front" + "ab"[core], [vmem] * 6, fields, [pair] + packed)(
            shift, own, halo, probe_at, kern, tables
        )

    def tail(core, own, halo, psi):
        body = functools.partial(tail_kernel, core)
        _, _, measured_at, shift = ready[core]
        return call(body, "tail" + "ab"[core], [vmem] * 6, (window, sums_of), deep)(
            shift, own, halo, psi, measured_at, tables
        )

    barrier = lax.optimization_barrier
    ready = [prepare(0), prepare(1)]
    psi_a = front(0, mine, first_a)
    g1_a, adj_a = tail(0, swapped, second_a, psi_a)
    spill_a1 = send("spill_a1", g1_a, rightward([(0, 1)]))
    g0_a = call(back_a_kernel, "backa", [vmem] * 4, window, [pair] + packed)(
        adj_a, *ready[0][:2], tables
    )
    spill_a0 = send("spill_a0", g0_a, rightward([(0, 1)]))
    first_b, g0_a = barrier((first_b, g0_a))
    psi_b = front(1, swapped, first_b)
    g1_b, adj_b = tail(1, mine, second_b, psi_b)
    spill_b1 = send("spill_b1", g1_b, rightward([(1, 0)]))
    give = call(back_b_kernel, "backb", [vmem] * 5, window, [pair] + packed)(
        adj_b, g1_a, *ready[1][:2], tables
    )
    spill_b0 = send("spill_b0", give, rightward([(1, 0)]))
    sums = jax.ShapeDtypeStruct((2, height, frame), F32)
    total = call(begin_kernel, "begin", [vmem] * 3, sums)(positions, g0_a, g1_b)
    total, give, spill_a1 = barrier((total, give, spill_a1))
    total = call(add_kernel, "add", [vmem] * 3, sums, aliases={1: 0}, cost=MEDIUM)(
        positions, total, spill_a1
    )
    total, give, spill_b1, spill_a0 = barrier((total, give, spill_b1, spill_a0))
    given = send("given", give, swap)
    trade = call(trade_kernel, "trade", [vmem] * 2, window)(spill_b1, spill_a0)
    traded = send("traded", trade, swap)
    out, _ = call(
        gather_kernel,
        "gather",
        [vmem] * 5,
        (jax.ShapeDtypeStruct(object_field.shape, BF), sums),
        [pltpu.VMEM((2, height, frame), BF), pltpu.SemaphoreType.DMA((2, height // frame))],
        out_specs=(hbm, vmem),
        aliases={1: 1},
    )(positions, total, spill_b0, traded, given)
    return out


def solution(mesh):
    placed = (P("depth", None, None, "pos"), P(), P(), P("pos", None, None), P())
    return jax.shard_map(
        functools.partial(local, mesh.shape["pos"]),
        mesh=mesh,
        in_specs=placed,
        out_specs=P("depth", None, None, "pos"),
        check_vma=False,
    )
```
